512 devices in a mesh: node: 4 (over z_lo, core), group: 32 (over x, y), fsdp: 4 (over z_hi).
Axes of the slice: x: 4, y: 8, z: 8 (z_hi: 4, z_lo: 2; z = z_hi * 2 + z_lo), core: 2. Of those that a mesh axis runs over, the one named last changes fastest.
Arguments:
- grad_values: bfloat16 [4, 32, 4, 128, 12288], P('node', 'group', 'fsdp'), may hold values from -6 to 6
- grad_scales: bfloat16 [4, 32, 4, 128, 96], P('node', 'group', 'fsdp'), may hold values from 0.5 to 4
- master: float32 [4, 128, 12288], P('fsdp', 'group'), may hold values from -6 to 6
- first_moment: bfloat16 [4, 128, 12288], P('fsdp', 'group'), may hold values from -1 to 1
- first_scale: float32 [4, 128, 96], P('fsdp', 'group'), may hold values from 0.5 to 2
- second_moment: bfloat16 [4, 128, 12288], P('fsdp', 'group'), may hold values from 0.049804688 to 1
- second_scale: float32 [4, 128, 96], P('fsdp', 'group'), may hold values from 10 to 100
Outputs:
- new_master: float32 [4, 128, 12288], P('fsdp', 'group')
- new_first: bfloat16 [4, 128, 12288], P('fsdp', 'group')
- new_first_scale: float32 [4, 128, 96], P('fsdp', 'group')
- new_second: bfloat16 [4, 128, 12288], P('fsdp', 'group')
- new_second_scale: float32 [4, 128, 96], P('fsdp', 'group')
- weights: bfloat16 [4, 128, 12288], P('fsdp')
- transposed: bfloat16 [4, 12288, 128], P('fsdp')
The draws below stay inside these ranges and needn't reach their ends.
All inputs are finite; a program needn't handle non-finite values. Where the reference program divides by a largest or mean magnitude, that divisor is 1e-20 or more.
Results may differ from the reference program's by a relative error of at most 0.001.
Values may be sent and summed in bfloat16 or wider, within the bound.
No kernel may reach another device: no remote copies, remote signals or barrier semaphores. Data moves between devices by JAX's collectives and lax.ppermute only.
A program may use at most 128 MiB of HBM per device.

```python
import math
import jax
import jax.numpy as jnp
from jax import lax

D = 12288
BLOCK = 128
ROWS_SHARD = 128
N_NODE = 4
N_GROUP = 32
N_FSDP = 4


def strengthened(values, key, source, target, shards_of, factor):
    owner, partner = [(jnp.arange(values.shape[position]) // (values.shape[position] // shards_of)).reshape([-1 if axis == position else 1 for axis in range(values.ndim)]) for position in (source, target)]
    chosen = jax.random.permutation(key, shards_of)[partner]
    strong = (owner == chosen) | (owner == (partner + shards_of // 2) % shards_of)
    return jnp.where(strong, factor * values, values)


def level_of(own_key, dims, cuts, least, largest):
    def one(position, parts):
        heights = jax.random.uniform(jax.random.fold_in(jax.random.fold_in(own_key, 6), position), (parts,), jnp.float32, least / len(cuts), largest / len(cuts))
        return jnp.repeat(jnp.exp(heights), dims[position] // parts).reshape((-1,) + (1,) * (len(dims) - position - 1))

    factor_of = one(*cuts[0])
    for cut in cuts[1:]:
        factor_of = factor_of * one(*cut)
    return factor_of


def bell_draw(own_key, shape, deviation, bound, cuts=(), held_as=jnp.bfloat16):
    factor_of = level_of(own_key, shape, cuts, -0.22, 0.18) if cuts else 1.0
    drawn = jax.random.normal(own_key, shape, jnp.float32) * deviation * factor_of
    return jnp.minimum(jnp.maximum(drawn, -bound), bound).astype(held_as)


def noise_with(stream_key, extent, deviation, limit, split, heavy, dtype=jnp.bfloat16):
    values = deviation * jax.random.normal(stream_key, extent, jnp.float32)
    if split:
        values = values * level_of(stream_key, extent, split, -0.22, 0.18)
    return jnp.clip(strengthened(values, jax.random.fold_in(stream_key, 3), *heavy), -limit, limit).astype(dtype)


def setup_inputs(seed: int = 0) -> dict:
    streams_of = jax.random.split(jax.random.key(seed), 8)
    return {
        "grad_values": noise_with(streams_of[0], (N_NODE, N_GROUP, N_FSDP, ROWS_SHARD, D), 1.0, 6.0, ((0, 4), (1, 32), (2, 4)), (1, 3, 32, 2.75)),
        "grad_scales": jnp.clip(jnp.exp(math.log(4.0) - 2.0794415 * jax.random.uniform(streams_of[1], (N_NODE, N_GROUP, N_FSDP, ROWS_SHARD, D // BLOCK), jnp.float32) ** level_of(streams_of[1], (N_NODE, N_GROUP, N_FSDP, ROWS_SHARD, D // BLOCK), ((0, 4), (1, 32), (2, 4)), -0.2, 0.2)), 0.5, 4.0).astype(jnp.bfloat16),
        "master": bell_draw(streams_of[2], (N_FSDP, ROWS_SHARD, D), 1.0, 6.0, ((0, 4), (1, 32)), jnp.float32),
        "first_moment": jnp.clip(jax.random.uniform(streams_of[3], (N_FSDP, ROWS_SHARD, D), jnp.float32, -1.0, 1.0) * level_of(streams_of[3], (N_FSDP, ROWS_SHARD, D), ((0, 4), (1, 32)), -0.4, 0.0), -1.0, 1.0).astype(jnp.bfloat16),
        "first_scale": jnp.clip(jnp.exp(math.log(2.0) - 1.3862944 * jax.random.uniform(streams_of[4], (N_FSDP, ROWS_SHARD, D // BLOCK), jnp.float32) ** level_of(streams_of[4], (N_FSDP, ROWS_SHARD, D // BLOCK), ((0, 4), (1, 32)), -0.2, 0.2)), 0.5, 2.0),
        "second_moment": jnp.clip(0.049804688 + 0.9501953 * jax.random.uniform(streams_of[5], (N_FSDP, ROWS_SHARD, D), jnp.float32) ** level_of(streams_of[5], (N_FSDP, ROWS_SHARD, D), ((0, 4), (1, 32)), -0.2, 0.2), 0.049804688, 1.0).astype(jnp.bfloat16),
        "second_scale": jnp.clip(jnp.exp(math.log(100.0) - 2.3025851 * jax.random.uniform(streams_of[6], (N_FSDP, ROWS_SHARD, D // BLOCK), jnp.float32) ** level_of(streams_of[6], (N_FSDP, ROWS_SHARD, D // BLOCK), ((0, 4), (1, 32)), -0.2, 0.2)), 10.0, 100.0),
    }


beta_one = 0.9
beta_two = 0.95
rate = 0.02
adam_eps = 1e-08
scale_eps = 1e-06
corr_one = 1.0 - 0.9 ** 10
corr_two = 1.0 - 0.95 ** 10

def expand(values, scales):
    shape = values.shape
    blocks = values.astype(jnp.float32).reshape(shape[:-1] + (shape[-1] // BLOCK, BLOCK))
    return (blocks * scales.astype(jnp.float32)[..., None]).reshape(shape)

def quantize(values, signed):
    shape = values.shape
    blocks = values.reshape(shape[:-1] + (shape[-1] // BLOCK, BLOCK))
    if signed:
        peak = lax.optimization_barrier(jnp.max(jnp.abs(blocks), axis=-1)) + scale_eps
    else:
        peak = lax.optimization_barrier(jnp.max(blocks, axis=-1)) + scale_eps
    coded = (blocks / peak[..., None]).astype(jnp.bfloat16).reshape(shape)
    return (coded, peak)

def adam_step(gradient, master, first_moment, first_scale, second_moment, second_scale):
    first = beta_one * expand(first_moment, first_scale) + (1.0 - beta_one) * gradient
    second = beta_two * expand(second_moment, second_scale) + (1.0 - beta_two) * gradient * gradient
    direction = first / corr_one / (jnp.sqrt(second / corr_two) + adam_eps)
    updated = master - rate * direction
    first_coded, first_peak = quantize(first, True)
    second_coded, second_peak = quantize(second, False)
    return (updated, first_coded, first_peak, second_coded, second_peak, updated.astype(jnp.bfloat16))

def reference(grad_values, grad_scales, master, first_moment, first_scale, second_moment, second_scale):
    count = grad_values.shape[0] * grad_values.shape[1]
    flat_values = grad_values.reshape((count,) + grad_values.shape[2:])
    flat_scales = grad_scales.reshape((count,) + grad_scales.shape[2:])

    def accumulate(total, pair):
        return (total + expand(pair[0], pair[1]), None)
    start = jnp.zeros(grad_values.shape[2:], jnp.float32)
    gradient, unused = lax.scan(accumulate, start, (flat_values, flat_scales))
    result = adam_step(gradient, master, first_moment, first_scale, second_moment, second_scale)
    updated, first_coded, first_peak, second_coded, second_peak, weights = result
    transposed = jnp.swapaxes(weights, 1, 2)
    return (updated, first_coded, first_peak, second_coded, second_peak, weights, transposed)
```

```python
import functools

import jax
import jax.numpy as jnp
from jax import lax
from jax.experimental import pallas as pl
from jax.experimental.pallas import tpu as pltpu
from jax.sharding import Mesh, PartitionSpec as P

D = 12288
HALF = D // 2
BLOCK = 128
NB = D // BLOCK
HB = NB // 2
ROWS = 128
NX, NY, NZ = 4, 8, 2
XR = ROWS // NX
YR = XR // NY
PAD = D + BLOCK
CH = 1024

beta_one = 0.9
beta_two = 0.95
rate = 0.02
adam_eps = 1e-08
scale_eps = 1e-06
corr_one = 1.0 - 0.9**10
corr_two = 1.0 - 0.95**10

f32 = jnp.float32
bf16 = jnp.bfloat16


def params(mib=48):
    return pltpu.CompilerParams(vmem_limit_bytes=mib * 1024 * 1024)


def cost(flops, nbytes):
    return pl.CostEstimate(flops=flops, bytes_accessed=nbytes, transcendentals=0)


def pack_kernel(idx, values, scales, out):
    out[:, :D] = values[...]
    out[:, D : D + NB] = scales[...]
    out[:, D + NB :] = jnp.zeros((XR, PAD - D - NB), bf16)


def pack(block, values, scales):
    return pl.pallas_call(
        pack_kernel,
        grid_spec=pltpu.PrefetchScalarGridSpec(
            num_scalar_prefetch=1,
            grid=(1,),
            in_specs=[
                pl.BlockSpec((XR, D), lambda i, s: (s[0], 0)),
                pl.BlockSpec((XR, NB), lambda i, s: (s[0], 0)),
            ],
            out_specs=pl.BlockSpec((XR, PAD), lambda i, s: (0, 0)),
        ),
        out_shape=jax.ShapeDtypeStruct((XR, PAD), bf16),
        compiler_params=params(),
        cost_estimate=cost(0, 2 * XR * D * 2),
        name="pack_rows",
    )(block, values, scales)


def sum_kernel(idx, v0, s0, v1, s1, v2, s2, v3, s3, out):
    first_half = idx[1] == 0
    scales = []
    for ref in (s0, s1, s2, s3):
        both = ref[...].astype(f32)
        scales.append(jnp.where(first_half, both[:, :HB], both[:, HB:NB]))
    for b in range(HB):
        cols = slice(b * BLOCK, (b + 1) * BLOCK)
        total = None
        for ref, scale in zip((v0, v1, v2, v3), scales):
            term = ref[:, cols].astype(f32) * scale[:, b : b + 1]
            total = term if total is None else total + term
        for i in range(NY):
            out[i, :, cols] = total[i * YR : (i + 1) * YR, :]


def sum_half(idx, values, scales, arrived):
    value_spec = pl.BlockSpec((XR, HALF), lambda i, s: (0, s[1]))
    scale_spec = pl.BlockSpec((XR, BLOCK), lambda i, s: (0, NB))
    ins = [
        pl.BlockSpec((XR, HALF), lambda i, s: (s[0], s[1])),
        pl.BlockSpec((XR, NB), lambda i, s: (s[0], 0)),
    ]
    args = [values, scales]
    for a in arrived:
        ins += [value_spec, scale_spec]
        args += [a, a]
    return pl.pallas_call(
        sum_kernel,
        grid_spec=pltpu.PrefetchScalarGridSpec(
            num_scalar_prefetch=1,
            grid=(1,),
            in_specs=ins,
            out_specs=pl.BlockSpec((NY, YR, HALF), lambda i, s: (0, 0, 0)),
        ),
        out_shape=jax.ShapeDtypeStruct((NY, YR, HALF), f32),
        compiler_params=params(),
        cost_estimate=cost(8 * XR * HALF, 12 * XR * HALF),
        name="sum_over_x",
    )(idx, *args)


def adam(gradient, master, first_old, second_old):
    first = beta_one * first_old + (1.0 - beta_one) * gradient
    second = beta_two * second_old + (1.0 - beta_two) * gradient * gradient
    direction = first / corr_one / (jnp.sqrt(second / corr_two) + adam_eps)
    return first, second, master - rate * direction


def low_kernel(idx, g0, g1, master, fm, fs, sm, ss, grad_out, low_out):
    first_half = idx[0] == 0
    fsv, ssv = fs[...], ss[...]
    fscale = jnp.where(first_half, fsv[:, :HB], fsv[:, HB:])
    sscale = jnp.where(first_half, ssv[:, :HB], ssv[:, HB:])
    for b in range(HB):
        cols = slice(b * BLOCK, (b + 1) * BLOCK)
        gradient = g0[:, cols] + g1[:, cols]
        grad_out[:, cols] = gradient
        first_old = fm[:, cols].astype(f32) * fscale[:, b : b + 1]
        second_old = sm[:, cols].astype(f32) * sscale[:, b : b + 1]
        _, _, updated = adam(gradient, master[:, cols], first_old, second_old)
        low = updated.astype(bf16)
        for i in range(NY):
            low_out[i, :, cols] = low


def low_weights(core, g0, g1, master, fm, fs, sm, ss):
    half = pl.BlockSpec((YR, HALF), lambda i, s: (0, s[0]))
    whole = pl.BlockSpec((YR, HALF), lambda i, s: (0, 0))
    scale = pl.BlockSpec((YR, NB), lambda i, s: (0, 0))
    return pl.pallas_call(
        low_kernel,
        grid_spec=pltpu.PrefetchScalarGridSpec(
            num_scalar_prefetch=1,
            grid=(1,),
            in_specs=[whole, whole, half, half, scale, half, scale],
            out_specs=[whole, pl.BlockSpec((NY, YR, HALF), lambda i, s: (0, 0, 0))],
        ),
        out_shape=[
            jax.ShapeDtypeStruct((YR, HALF), f32),
            jax.ShapeDtypeStruct((NY, YR, HALF), bf16),
        ],
        compiler_params=params(),
        cost_estimate=cost(30 * YR * HALF, 40 * YR * HALF),
        name="low_weights",
    )(core, g0, g1, master, fm, fs, sm, ss)


def state_kernel(idx, mine, other, master, fm, fs, sm, ss, om, of, ofs, os, oss):
    first_half = idx[0] == 0
    fsv, ssv = fs[...], ss[...]
    lane = lax.broadcasted_iota(jnp.int32, (YR, NB), 1)
    fpeaks = jnp.zeros((YR, NB), f32)
    speaks = jnp.zeros((YR, NB), f32)
    for b in range(NB):
        cols = slice(b * BLOCK, (b + 1) * BLOCK)
        inner = slice((b % HB) * BLOCK, (b % HB + 1) * BLOCK)
        one, two = (mine, other) if b < HB else (other, mine)
        gradient = jnp.where(first_half, one[:, inner], two[:, inner])
        first_old = fm[:, cols].astype(f32) * fsv[:, b : b + 1]
        second_old = sm[:, cols].astype(f32) * ssv[:, b : b + 1]
        first, second, updated = adam(gradient, master[:, cols], first_old, second_old)
        om[:, cols] = updated
        fpeak = jnp.max(jnp.abs(first), axis=1, keepdims=True) + scale_eps
        speak = jnp.max(second, axis=1, keepdims=True) + scale_eps
        of[:, cols] = (first / fpeak).astype(bf16)
        os[:, cols] = (second / speak).astype(bf16)
        fpeaks = jnp.where(lane == b, fpeak, fpeaks)
        speaks = jnp.where(lane == b, speak, speaks)
    ofs[...] = fpeaks
    oss[...] = speaks


def states(core, mine, other, master, fm, fs, sm, ss):
    half = pl.BlockSpec((YR, HALF), lambda i, s: (0, 0))
    whole = pl.BlockSpec((YR, D), lambda i, s: (0, 0))
    scale = pl.BlockSpec((YR, NB), lambda i, s: (0, 0))
    shape = jax.ShapeDtypeStruct
    return pl.pallas_call(
        state_kernel,
        grid_spec=pltpu.PrefetchScalarGridSpec(
            num_scalar_prefetch=1,
            grid=(1,),
            in_specs=[half, half, whole, whole, scale, whole, scale],
            out_specs=[whole, whole, scale, whole, scale],
        ),
        out_shape=[
            shape((YR, D), f32),
            shape((YR, D), bf16),
            shape((YR, NB), f32),
            shape((YR, D), bf16),
            shape((YR, NB), f32),
        ],
        compiler_params=params(),
        cost_estimate=cost(60 * YR * D, 20 * YR * D),
        name="new_states",
    )(core, mine, other, master, fm, fs, sm, ss)


def place_kernel(idx, *refs):
    pieces, (weights, transposed, rows) = refs[:8], refs[8:]
    x = idx[0]

    def place(group):
        for shift, ref in enumerate(group):
            start = pl.multiple_of(lax.rem(x + NX - shift, NX) * XR, XR)
            rows[pl.ds(start, XR), :] = ref[...].astype(f32).reshape(XR, CH)

    @pl.when(pl.program_id(0) == 0)
    def _():
        place(pieces[:4])

    @pl.when(pl.program_id(0) == 1)
    def _():
        place(pieces[4:])

    low = rows[...]
    weights[...] = low.astype(bf16)
    transposed[...] = low.T.astype(bf16)


def place_all(idx, mine, other):
    steps = HALF // CH
    first = pl.BlockSpec(
        (NY, YR, CH), lambda h, j, s: (0, 0, jnp.where(h == 0, j, steps - 1))
    )
    second = pl.BlockSpec((NY, YR, CH), lambda h, j, s: (0, 0, jnp.where(h == 0, 0, j)))

    def column(h, j, s):
        return jnp.where(h == 0, s[1], 1 - s[1]) * steps + j

    return pl.pallas_call(
        place_kernel,
        grid_spec=pltpu.PrefetchScalarGridSpec(
            num_scalar_prefetch=1,
            grid=(2, steps),
            in_specs=[first] * 4 + [second] * 4,
            out_specs=[
                pl.BlockSpec((ROWS, CH), lambda h, j, s: (0, column(h, j, s))),
                pl.BlockSpec((CH, ROWS), lambda h, j, s: (column(h, j, s), 0)),
            ],
            scratch_shapes=[pltpu.VMEM((ROWS, CH), f32)],
        ),
        out_shape=[
            jax.ShapeDtypeStruct((ROWS, D), bf16),
            jax.ShapeDtypeStruct((D, ROWS), bf16),
        ],
        compiler_params=params(),
        cost_estimate=cost(0, 3 * ROWS * D * 2),
        name="place_weights",
    )(idx, *mine, *other)


def shift_x(value, shift):
    return lax.ppermute(value, "x", [(i, (i + shift) % NX) for i in range(NX)])


def swap(value, axis):
    return lax.ppermute(value, axis, [(0, 1), (1, 0)])


def on_device(gv, gs, master, fm, fs, sm, ss):
    gv, gs = gv.reshape(ROWS, D), gs.reshape(ROWS, NB)
    master, fm, sm = master.reshape(YR, D), fm.reshape(YR, D), sm.reshape(YR, D)
    fs, ss = fs.reshape(YR, NB), ss.reshape(YR, NB)
    x = lax.axis_index("x").astype(jnp.int32)
    core = lax.axis_index("c").astype(jnp.int32)

    arrived = []
    for shift in (2, 1, 3):
        block = lax.rem(x + shift, NX).reshape(1)
        arrived.append(shift_x(pack(block, gv, gs), shift))
    theirs = sum_half(jnp.stack([x, 1 - core]), gv, gs, arrived)
    from_core = swap(theirs, "c")
    ours = sum_half(jnp.stack([x, core]), gv, gs, arrived)
    chip = ours + from_core
    plane = jnp.sum(lax.all_to_all(chip, "y", 0, 0, tiled=True), axis=0)
    from_z = swap(plane, "zl")
    gradient, low = low_weights(
        core.reshape(1), plane, from_z, master, fm, fs, sm, ss
    )
    low_y = lax.all_to_all(low, "y", 0, 0, tiled=True)
    other_gradient = swap(gradient, "c")
    new = states(core.reshape(1), gradient, other_gradient, master, fm, fs, sm, ss)
    mine = [low_y, shift_x(low_y, 1), shift_x(low_y, 2), shift_x(low_y, 3)]
    other = [swap(piece, "c") for piece in mine]
    weights, transposed = place_all(jnp.stack([x, core]), mine, other)
    om, of, ofs, os, oss = [a[None] for a in new]
    return om, of, ofs, os, oss, weights[None], transposed[None]


def solution(mesh):
    fine = Mesh(
        mesh.devices.reshape(NZ, 2, NX, NY, mesh.devices.shape[-1]),
        ("zl", "c", "x", "y", "zh"),
    )
    grads = P(("zl", "c"), ("x", "y"), "zh", None, None)
    rows = P("zh", ("x", "y"), None)
    shard = P("zh", None, None)
    return jax.shard_map(
        on_device,
        mesh=fine,
        in_specs=(grads, grads, rows, rows, rows, rows, rows),
        out_specs=(rows,) * 5 + (shard, shard),
        check_vma=False,
    )
```

```python
import functools

import jax
import jax.numpy as jnp
from jax import lax
from jax.experimental import pallas as pl
from jax.experimental.pallas import tpu as pltpu
from jax.sharding import Mesh, PartitionSpec as P

D = 12288
HALF = D // 2
BLOCK = 128
NB = D // BLOCK
HB = NB // 2
ROWS = 128
NX, NY, NZ = 4, 8, 2
XR = ROWS // NX
YR = XR // NY
PAD = HALF + BLOCK
SPAN = 172.0
OFFSET = 86.0
CH = 3072

beta_one = 0.9
beta_two = 0.95
rate = 0.02
adam_eps = 1e-08
scale_eps = 1e-06
corr_one = 1.0 - 0.9**10
corr_two = 1.0 - 0.95**10

f32 = jnp.float32
bf16 = jnp.bfloat16


def params(mib=48):
    return pltpu.CompilerParams(vmem_limit_bytes=mib * 1024 * 1024)


def cost(flops, nbytes):
    return pl.CostEstimate(flops=flops, bytes_accessed=nbytes, transcendentals=0)


def encode(value, factor):
    size = jnp.exp(jnp.abs(value) * factor - OFFSET)
    return jnp.where(value < 0, -size, size)


def decode(code, step):
    size = (jnp.log(jnp.abs(code)) + OFFSET) * step
    return jnp.where(code < 0, -size, size)


def scale_of(peak):
    return jnp.maximum(peak * (1.0 + 2.0**-7), 1e-30).astype(bf16)


def half_of(scales, first_half):
    return jnp.where(first_half, scales[:, :HB], scales[:, HB:NB])


def pack_kernel(idx, values, scales, out):
    out[:, :HALF] = values[...]
    both = scales[...].astype(f32)
    chosen = half_of(both, idx[0] == 0).astype(bf16)
    out[:, HALF : HALF + HB] = chosen
    out[:, HALF + HB :] = jnp.zeros((XR, BLOCK - HB), bf16)


def pack(half, values, scales):
    return pl.pallas_call(
        pack_kernel,
        grid_spec=pltpu.PrefetchScalarGridSpec(
            num_scalar_prefetch=1,
            grid=(NX,),
            in_specs=[
                pl.BlockSpec((XR, HALF), lambda i, s: (i, s[0])),
                pl.BlockSpec((XR, NB), lambda i, s: (i, 0)),
            ],
            out_specs=pl.BlockSpec((XR, PAD), lambda i, s: (i, 0)),
        ),
        out_shape=jax.ShapeDtypeStruct((ROWS, PAD), bf16),
        compiler_params=params(62),
        cost_estimate=cost(0, 2 * ROWS * HALF * 2),
        name="pack_rows",
    )(half, values, scales)


def chip_kernel(idx, values, scales, there, there_scales, out, totals):
    mine = half_of(scales[...].astype(f32), idx[1] == 0)
    theirs = there_scales[...].astype(f32)
    peak = jnp.zeros((XR, BLOCK), f32)
    for b in range(HB):
        cols = slice(b * BLOCK, (b + 1) * BLOCK)
        total = values[:, cols].astype(f32) * mine[:, b : b + 1]
        total = total + there[:, cols].astype(f32) * theirs[:, b : b + 1]
        totals[:, cols] = total
        peak = jnp.maximum(peak, jnp.abs(total))
    scale = scale_of(peak)
    out[:, HALF:] = scale
    factor = SPAN / scale.astype(f32)
    for b in range(HB):
        cols = slice(b * BLOCK, (b + 1) * BLOCK)
        out[:, cols] = encode(totals[:, cols], factor).astype(bf16)


def chip_sum(idx, values, scales, there):
    return pl.pallas_call(
        chip_kernel,
        grid_spec=pltpu.PrefetchScalarGridSpec(
            num_scalar_prefetch=1,
            grid=(1,),
            in_specs=[
                pl.BlockSpec((XR, HALF), lambda i, s: (s[0], s[1])),
                pl.BlockSpec((XR, NB), lambda i, s: (s[0], 0)),
                pl.BlockSpec((XR, HALF), lambda i, s: (s[0], 0)),
                pl.BlockSpec((XR, BLOCK), lambda i, s: (s[0], HB)),
            ],
            out_specs=pl.BlockSpec((XR, PAD), lambda i, s: (0, 0)),
            scratch_shapes=[pltpu.VMEM((XR, HALF), f32)],
        ),
        out_shape=jax.ShapeDtypeStruct((XR, PAD), bf16),
        compiler_params=params(),
        cost_estimate=cost(20 * XR * HALF, 6 * XR * HALF),
        name="sum_on_chip",
    )(idx, values, scales, there, there)


def row_kernel(
    idx, values, scales, there, there_scales, c1, s1, c2, s2, c3, s3, out, totals
):
    mine = half_of(scales[...].astype(f32), idx[1] == 0)
    theirs = there_scales[...].astype(f32)
    coded = [
        (ref, scale[...].astype(f32) * (1.0 / SPAN))
        for ref, scale in ((c1, s1), (c2, s2), (c3, s3))
    ]
    peak = jnp.zeros((XR, BLOCK), f32)
    for b in range(HB):
        cols = slice(b * BLOCK, (b + 1) * BLOCK)
        total = values[:, cols].astype(f32) * mine[:, b : b + 1]
        total = total + there[:, cols].astype(f32) * theirs[:, b : b + 1]
        for ref, step in coded:
            total = total + decode(ref[:, cols].astype(f32), step)
        totals[:, cols] = total
        peak = jnp.maximum(peak, jnp.abs(total))
    scale = scale_of(peak).astype(f32)
    out[:, :, HALF:] = scale.reshape(NY, YR, BLOCK).astype(bf16)
    factor = SPAN / scale
    for b in range(HB):
        cols = slice(b * BLOCK, (b + 1) * BLOCK)
        code = encode(totals[:, cols], factor)
        out[:, :, cols] = code.reshape(NY, YR, BLOCK).astype(bf16)


def row_sum(idx, values, scales, there, arrived):
    ins = [
        pl.BlockSpec((XR, HALF), lambda i, s: (s[0], s[1])),
        pl.BlockSpec((XR, NB), lambda i, s: (s[0], 0)),
        pl.BlockSpec((XR, HALF), lambda i, s: (s[0], 0)),
        pl.BlockSpec((XR, BLOCK), lambda i, s: (s[0], HB)),
    ]
    args = [values, scales, there, there]
    for a in arrived:
        ins += [
            pl.BlockSpec((XR, HALF), lambda i, s: (0, 0)),
            pl.BlockSpec((XR, BLOCK), lambda i, s: (0, HB)),
        ]
        args += [a, a]
    return pl.pallas_call(
        row_kernel,
        grid_spec=pltpu.PrefetchScalarGridSpec(
            num_scalar_prefetch=1,
            grid=(1,),
            in_specs=ins,
            out_specs=pl.BlockSpec((NY, YR, PAD), lambda i, s: (0, 0, 0)),
            scratch_shapes=[pltpu.VMEM((XR, HALF), f32)],
        ),
        out_shape=jax.ShapeDtypeStruct((NY, YR, PAD), bf16),
        compiler_params=params(),
        cost_estimate=cost(60 * XR * HALF, 12 * XR * HALF),
        name="sum_over_x",
    )(idx, *args)


def plane_kernel(codes, scales, out):
    step = scales[...].astype(f32).reshape(XR, BLOCK) * (1.0 / SPAN)
    for b in range(HB):
        cols = slice(b * BLOCK, (b + 1) * BLOCK)
        code = codes[:, :, cols].astype(f32).reshape(XR, BLOCK)
        term = decode(code, step)
        out[:, cols] = jnp.sum(term.reshape(NY, YR, BLOCK), axis=0)


def plane_sum(codes):
    return pl.pallas_call(
        plane_kernel,
        grid=(1,),
        in_specs=[
            pl.BlockSpec((NY, YR, HALF), lambda i: (0, 0, 0)),
            pl.BlockSpec((NY, YR, BLOCK), lambda i: (0, 0, HB)),
        ],
        out_specs=pl.BlockSpec((YR, HALF), lambda i: (0, 0)),
        out_shape=jax.ShapeDtypeStruct((YR, HALF), f32),
        compiler_params=params(),
        cost_estimate=cost(20 * XR * HALF, 3 * XR * HALF),
        name="sum_over_y",
    )(codes, codes)


def adam(gradient, master, first_old, second_old):
    first = beta_one * first_old + (1.0 - beta_one) * gradient
    second = beta_two * second_old + (1.0 - beta_two) * gradient * gradient
    direction = first / corr_one / (jnp.sqrt(second / corr_two) + adam_eps)
    return first, second, master - rate * direction


def low_kernel(idx, g0, g1, master, fm, fs, sm, ss, grad_out, low_out):
    first_half = idx[0] == 0
    fsv, ssv = fs[...], ss[...]
    fscale = jnp.where(first_half, fsv[:, :HB], fsv[:, HB:])
    sscale = jnp.where(first_half, ssv[:, :HB], ssv[:, HB:])
    for b in range(HB):
        cols = slice(b * BLOCK, (b + 1) * BLOCK)
        gradient = g0[:, cols] + g1[:, cols]
        grad_out[:, cols] = gradient
        first_old = fm[:, cols].astype(f32) * fscale[:, b : b + 1]
        second_old = sm[:, cols].astype(f32) * sscale[:, b : b + 1]
        _, _, updated = adam(gradient, master[:, cols], first_old, second_old)
        low = updated.astype(bf16)
        for i in range(NY):
            low_out[i, :, cols] = low


def low_weights(core, g0, g1, master, fm, fs, sm, ss):
    half = pl.BlockSpec((YR, HALF), lambda i, s: (0, s[0]))
    whole = pl.BlockSpec((YR, HALF), lambda i, s: (0, 0))
    scale = pl.BlockSpec((YR, NB), lambda i, s: (0, 0))
    return pl.pallas_call(
        low_kernel,
        grid_spec=pltpu.PrefetchScalarGridSpec(
            num_scalar_prefetch=1,
            grid=(1,),
            in_specs=[whole, whole, half, half, scale, half, scale],
            out_specs=[whole, pl.BlockSpec((NY, YR, HALF), lambda i, s: (0, 0, 0))],
        ),
        out_shape=[
            jax.ShapeDtypeStruct((YR, HALF), f32),
            jax.ShapeDtypeStruct((NY, YR, HALF), bf16),
        ],
        compiler_params=params(),
        cost_estimate=cost(30 * YR * HALF, 40 * YR * HALF),
        name="low_weights",
    )(core, g0, g1, master, fm, fs, sm, ss)


def state_kernel(idx, mine, other, master, fm, fs, sm, ss, om, of, ofs, os, oss):
    first_half = idx[0] == 0
    fsv, ssv = fs[...], ss[...]
    lane = lax.broadcasted_iota(jnp.int32, (YR, NB), 1)
    fpeaks = jnp.zeros((YR, NB), f32)
    speaks = jnp.zeros((YR, NB), f32)
    for b in range(NB):
        cols = slice(b * BLOCK, (b + 1) * BLOCK)
        inner = slice((b % HB) * BLOCK, (b % HB + 1) * BLOCK)
        one, two = (mine, other) if b < HB else (other, mine)
        gradient = jnp.where(first_half, one[:, inner], two[:, inner])
        first_old = fm[:, cols].astype(f32) * fsv[:, b : b + 1]
        second_old = sm[:, cols].astype(f32) * ssv[:, b : b + 1]
        first, second, updated = adam(gradient, master[:, cols], first_old, second_old)
        om[:, cols] = updated
        fpeak = jnp.max(jnp.abs(first), axis=1, keepdims=True) + scale_eps
        speak = jnp.max(second, axis=1, keepdims=True) + scale_eps
        of[:, cols] = (first / fpeak).astype(bf16)
        os[:, cols] = (second / speak).astype(bf16)
        fpeaks = jnp.where(lane == b, fpeak, fpeaks)
        speaks = jnp.where(lane == b, speak, speaks)
    ofs[...] = fpeaks
    oss[...] = speaks


def states(core, mine, other, master, fm, fs, sm, ss):
    half = pl.BlockSpec((YR, HALF), lambda i, s: (0, 0))
    whole = pl.BlockSpec((YR, D), lambda i, s: (0, 0))
    scale = pl.BlockSpec((YR, NB), lambda i, s: (0, 0))
    shape = jax.ShapeDtypeStruct
    return pl.pallas_call(
        state_kernel,
        grid_spec=pltpu.PrefetchScalarGridSpec(
            num_scalar_prefetch=1,
            grid=(1,),
            in_specs=[half, half, whole, whole, scale, whole, scale],
            out_specs=[whole, whole, scale, whole, scale],
        ),
        out_shape=[
            shape((YR, D), f32),
            shape((YR, D), bf16),
            shape((YR, NB), f32),
            shape((YR, D), bf16),
            shape((YR, NB), f32),
        ],
        compiler_params=params(),
        cost_estimate=cost(60 * YR * D, 20 * YR * D),
        name="new_states",
    )(core, mine, other, master, fm, fs, sm, ss)


def place_kernel(idx, *refs):
    pieces, (weights, transposed, rows) = refs[:8], refs[8:]
    x = idx[0]

    def place(group):
        for shift, ref in enumerate(group):
            start = pl.multiple_of(lax.rem(x + NX - shift, NX) * XR, XR)
            rows[pl.ds(start, XR), :] = ref[...].astype(f32).reshape(XR, CH).astype(bf16)

    @pl.when(pl.program_id(0) == 0)
    def _():
        place(pieces[:4])

    @pl.when(pl.program_id(0) == 1)
    def _():
        place(pieces[4:])

    low = rows[...]
    weights[...] = low
    transposed[...] = low.T


def place_all(idx, mine, other):
    steps = HALF // CH
    first = pl.BlockSpec(
        (NY, YR, CH), lambda h, j, s: (0, 0, jnp.where(h == 0, j, steps - 1))
    )
    second = pl.BlockSpec((NY, YR, CH), lambda h, j, s: (0, 0, jnp.where(h == 0, 0, j)))

    def column(h, j, s):
        return jnp.where(h == 0, s[1], 1 - s[1]) * steps + j

    return pl.pallas_call(
        place_kernel,
        grid_spec=pltpu.PrefetchScalarGridSpec(
            num_scalar_prefetch=1,
            grid=(2, steps),
            in_specs=[first] * 4 + [second] * 4,
            out_specs=[
                pl.BlockSpec((ROWS, CH), lambda h, j, s: (0, column(h, j, s))),
                pl.BlockSpec((CH, ROWS), lambda h, j, s: (column(h, j, s), 0)),
            ],
            scratch_shapes=[pltpu.VMEM((ROWS, CH), bf16)],
        ),
        out_shape=[
            jax.ShapeDtypeStruct((ROWS, D), bf16),
            jax.ShapeDtypeStruct((D, ROWS), bf16),
        ],
        compiler_params=params(),
        cost_estimate=cost(0, 3 * ROWS * D * 2),
        name="place_weights",
    )(idx, *mine, *other)


def shift_x(value, shift):
    return lax.ppermute(value, "x", [(i, (i + shift) % NX) for i in range(NX)])


def swap(value, axis):
    return lax.ppermute(value, axis, [(0, 1), (1, 0)])


def on_device(gv, gs, master, fm, fs, sm, ss):
    gv, gs = gv.reshape(ROWS, D), gs.reshape(ROWS, NB)
    master, fm, sm = master.reshape(YR, D), fm.reshape(YR, D), sm.reshape(YR, D)
    fs, ss = fs.reshape(YR, NB), ss.reshape(YR, NB)
    x = lax.axis_index("x").astype(jnp.int32)
    core = lax.axis_index("c").astype(jnp.int32)

    there = swap(pack(1 - core.reshape(1), gv, gs), "c")
    arrived = []
    for shift in (2, 1, 3):
        target = jnp.stack([lax.rem(x + shift, NX), core])
        arrived.append(shift_x(chip_sum(target, gv, gs, there), shift))
    codes = row_sum(jnp.stack([x, core]), gv, gs, there, arrived)
    plane = plane_sum(lax.all_to_all(codes, "y", 0, 0, tiled=True))
    from_z = swap(plane, "zl")
    gradient, low = low_weights(
        core.reshape(1), plane, from_z, master, fm, fs, sm, ss
    )
    low_y = lax.all_to_all(low, "y", 0, 0, tiled=True)
    mine = [low_y, shift_x(low_y, 1), shift_x(low_y, 2), shift_x(low_y, 3)]
    other_gradient = swap(gradient, "c")
    new = states(core.reshape(1), gradient, other_gradient, master, fm, fs, sm, ss)
    mine[1], new = lax.optimization_barrier((mine[1], new))
    other = [swap(piece, "c") for piece in mine]
    weights, transposed = place_all(jnp.stack([x, core]), mine, other)
    om, of, ofs, os, oss = [a[None] for a in new]
    return om, of, ofs, os, oss, weights[None], transposed[None]


def solution(mesh):
    fine = Mesh(
        mesh.devices.reshape(NZ, 2, NX, NY, mesh.devices.shape[-1]),
        ("zl", "c", "x", "y", "zh"),
    )
    grads = P(("zl", "c"), ("x", "y"), "zh", None, None)
    rows = P("zh", ("x", "y"), None)
    shard = P("zh", None, None)
    return jax.shard_map(
        on_device,
        mesh=fine,
        in_specs=(grads, grads, rows, rows, rows, rows, rows),
        out_specs=(rows,) * 5 + (shard, shard),
        check_vma=False,
    )
```

```python
import functools

import jax
import jax.numpy as jnp
from jax import lax
from jax.experimental import pallas as pl
from jax.experimental.pallas import tpu as pltpu
from jax.sharding import Mesh, PartitionSpec as P

D = 12288
HALF = D // 2
BLOCK = 128
NB = D // BLOCK
HB = NB // 2
ROWS = 128
NX, NY, NZ = 4, 8, 2
XR = ROWS // NX
YR = XR // NY
QUARTER = D // 4
QB = NB // 4
PAD = HALF + BLOCK
QPAD = QUARTER + BLOCK
SPAN = 172.0
OFFSET = 86.0

beta_one = 0.9
beta_two = 0.95
rate = 0.02
adam_eps = 1e-08
scale_eps = 1e-06
corr_one = 1.0 - 0.9**10
corr_two = 1.0 - 0.95**10

f32 = jnp.float32
bf16 = jnp.bfloat16


def params(mib=24):
    return pltpu.CompilerParams(vmem_limit_bytes=mib * 1024 * 1024)


def cost(flops, nbytes):
    return pl.CostEstimate(flops=flops, bytes_accessed=nbytes, transcendentals=0)


def encode(value, factor):
    size = jnp.exp(jnp.abs(value) * factor - OFFSET)
    return jnp.where(value < 0, -size, size)


def decode(code, step):
    size = (jnp.log(jnp.abs(code)) + OFFSET) * step
    return jnp.where(code < 0, -size, size)


def scale_of(peak):
    return jnp.maximum(peak * (1.0 + 2.0**-7), 1e-30).astype(bf16)


def pack_kernel(idx, values, scales, out, own):
    rows = scales[...].astype(f32).T
    low, high = rows[:, :HB], rows[:, HB:NB]
    pad = jnp.zeros((ROWS, BLOCK - HB), bf16)
    first = idx[0] == 0
    out[:, :HALF] = values[...]
    out[:, HALF : HALF + HB] = jnp.where(first, low, high).astype(bf16)
    out[:, HALF + HB :] = pad
    own[:, :HB] = jnp.where(first, high, low).astype(bf16)
    own[:, HB:] = pad


def pack(half, values, scales):
    return pl.pallas_call(
        pack_kernel,
        grid_spec=pltpu.PrefetchScalarGridSpec(
            num_scalar_prefetch=1,
            grid=(1,),
            in_specs=[
                pl.BlockSpec((ROWS, HALF), lambda i, s: (0, s[0])),
                pl.BlockSpec((NB, ROWS), lambda i, s: (0, 0)),
            ],
            out_specs=[
                pl.BlockSpec((ROWS, PAD), lambda i, s: (0, 0)),
                pl.BlockSpec((ROWS, BLOCK), lambda i, s: (0, 0)),
            ],
        ),
        out_shape=[
            jax.ShapeDtypeStruct((ROWS, PAD), bf16),
            jax.ShapeDtypeStruct((ROWS, BLOCK), bf16),
        ],
        compiler_params=params(),
        cost_estimate=cost(0, 2 * ROWS * HALF * 2),
        name="pack_rows",
    )(half, values, scales)


def add_cores(values, scales, there, there_scales, totals):
    mine = scales[...].astype(f32)
    theirs = there_scales[...].astype(f32)
    peak = jnp.zeros((XR, BLOCK), f32)
    for b in range(HB):
        cols = slice(b * BLOCK, (b + 1) * BLOCK)
        total = values[:, cols].astype(f32) * mine[:, b : b + 1]
        total = total + there[:, cols].astype(f32) * theirs[:, b : b + 1]
        totals[:, cols] = total
        peak = jnp.maximum(peak, jnp.abs(total))
    return peak


def code_kernel(idx, values, scales, there, there_scales, out, totals):
    scale = scale_of(add_cores(values, scales, there, there_scales, totals))
    out[:, HALF:] = scale
    factor = SPAN / scale.astype(f32)
    for b in range(HB):
        cols = slice(b * BLOCK, (b + 1) * BLOCK)
        out[:, cols] = encode(totals[:, cols], factor).astype(bf16)


def own_kernel(idx, values, scales, there, there_scales, out):
    add_cores(values, scales, there, there_scales, out)


def chip_sum(idx, values, scales, there, coded):
    if coded:
        kernel, width, kind, name = code_kernel, PAD, bf16, "coded_chip_sum"
        scratch = [pltpu.VMEM((XR, HALF), f32)]
    else:
        kernel, width, kind, name = own_kernel, HALF, f32, "own_chip_sum"
        scratch = []
    return pl.pallas_call(
        kernel,
        grid_spec=pltpu.PrefetchScalarGridSpec(
            num_scalar_prefetch=1,
            grid=(1,),
            in_specs=[
                pl.BlockSpec((XR, HALF), lambda i, s: (s[0], s[1])),
                pl.BlockSpec((XR, BLOCK), lambda i, s: (s[0], 0)),
                pl.BlockSpec((XR, HALF), lambda i, s: (s[0], 0)),
                pl.BlockSpec((XR, BLOCK), lambda i, s: (s[0], HB)),
            ],
            out_specs=pl.BlockSpec((XR, width), lambda i, s: (0, 0)),
            scratch_shapes=scratch,
        ),
        out_shape=jax.ShapeDtypeStruct((XR, width), kind),
        compiler_params=params(),
        cost_estimate=cost(20 * XR * HALF, 6 * XR * HALF),
        name=name,
    )(idx, values, scales, there, there)


def row_kernel(own, c1, s1, c2, s2, c3, s3, out, totals):
    coded = [
        (ref, scale[...].astype(f32) * (1.0 / SPAN))
        for ref, scale in ((c1, s1), (c2, s2), (c3, s3))
    ]
    peak = jnp.zeros((XR, BLOCK), f32)
    for b in range(HB):
        cols = slice(b * BLOCK, (b + 1) * BLOCK)
        total = own[:, cols]
        for ref, step in coded:
            total = total + decode(ref[:, cols].astype(f32), step)
        totals[:, cols] = total
        peak = jnp.maximum(peak, jnp.abs(total))
    scale = scale_of(peak).astype(f32)
    for z in range(NZ):
        planes = slice(z * NY, (z + 1) * NY)
        out[planes, :, QUARTER:] = scale.reshape(NY, YR, BLOCK).astype(bf16)
    factor = SPAN / scale
    for b in range(HB):
        cols = slice(b * BLOCK, (b + 1) * BLOCK)
        z, inner = b // QB, slice(b % QB * BLOCK, (b % QB + 1) * BLOCK)
        code = encode(totals[:, cols], factor)
        out[z * NY : (z + 1) * NY, :, inner] = code.reshape(NY, YR, BLOCK).astype(bf16)


def row_sum(own, arrived):
    ins = [pl.BlockSpec((XR, HALF), lambda i: (0, 0))]
    args = [own]
    for a in arrived:
        ins += [
            pl.BlockSpec((XR, HALF), lambda i: (0, 0)),
            pl.BlockSpec((XR, BLOCK), lambda i: (0, HB)),
        ]
        args += [a, a]
    return pl.pallas_call(
        row_kernel,
        grid=(1,),
        in_specs=ins,
        out_specs=pl.BlockSpec((NZ * NY, YR, QPAD), lambda i: (0, 0, 0)),
        scratch_shapes=[pltpu.VMEM((XR, HALF), f32)],
        out_shape=jax.ShapeDtypeStruct((NZ * NY, YR, QPAD), bf16),
        compiler_params=params(),
        cost_estimate=cost(60 * XR * HALF, 12 * XR * HALF),
        name="sum_over_x",
    )(*args)


def last_kernel(codes, scales, out):
    parts = NZ * NY * YR
    step = scales[...].astype(f32).reshape(parts, BLOCK) * (1.0 / SPAN)
    for b in range(QB):
        cols = slice(b * BLOCK, (b + 1) * BLOCK)
        code = codes[:, :, cols].astype(f32).reshape(parts, BLOCK)
        term = decode(code, step)
        out[:, cols] = jnp.sum(term.reshape(NZ * NY, YR, BLOCK), axis=0)


def last_sum(codes):
    return pl.pallas_call(
        last_kernel,
        grid=(1,),
        in_specs=[
            pl.BlockSpec((NZ * NY, YR, QUARTER), lambda i: (0, 0, 0)),
            pl.BlockSpec((NZ * NY, YR, BLOCK), lambda i: (0, 0, QB)),
        ],
        out_specs=pl.BlockSpec((YR, QUARTER), lambda i: (0, 0)),
        out_shape=jax.ShapeDtypeStruct((YR, QUARTER), f32),
        compiler_params=params(),
        cost_estimate=cost(20 * XR * HALF, 3 * XR * HALF),
        name="sum_over_zy",
    )(codes, codes)


def adam(gradient, master, first_old, second_old):
    first = beta_one * first_old + (1.0 - beta_one) * gradient
    second = beta_two * second_old + (1.0 - beta_two) * gradient * gradient
    direction = first / corr_one / (jnp.sqrt(second / corr_two) + adam_eps)
    return first, second, master - rate * direction


def low_kernel(idx, grad, master, fm, fs, sm, ss, low_out):
    def chosen(ref):
        scales = ref[...]
        parts = [scales[:, k * QB : (k + 1) * QB] for k in range(4)]
        low = jnp.where(idx[0] == 0, parts[0], parts[1])
        high = jnp.where(idx[0] == 2, parts[2], parts[3])
        return jnp.where(idx[0] < 2, low, high)

    fscale, sscale = chosen(fs), chosen(ss)
    for b in range(QB):
        cols = slice(b * BLOCK, (b + 1) * BLOCK)
        first_old = fm[:, cols].astype(f32) * fscale[:, b : b + 1]
        second_old = sm[:, cols].astype(f32) * sscale[:, b : b + 1]
        _, _, updated = adam(grad[:, cols], master[:, cols], first_old, second_old)
        low = updated.astype(bf16)
        for i in range(NZ * NY):
            low_out[i, :, cols] = low


def low_weights(quarter, grad, master, fm, fs, sm, ss):
    part = pl.BlockSpec((YR, QUARTER), lambda i, s: (0, s[0]))
    whole = pl.BlockSpec((YR, QUARTER), lambda i, s: (0, 0))
    scale = pl.BlockSpec((YR, NB), lambda i, s: (0, 0))
    return pl.pallas_call(
        low_kernel,
        grid_spec=pltpu.PrefetchScalarGridSpec(
            num_scalar_prefetch=1,
            grid=(1,),
            in_specs=[whole, part, part, scale, part, scale],
            out_specs=pl.BlockSpec((NZ * NY, YR, QUARTER), lambda i, s: (0, 0, 0)),
        ),
        out_shape=jax.ShapeDtypeStruct((NZ * NY, YR, QUARTER), bf16),
        compiler_params=params(),
        cost_estimate=cost(30 * YR * QUARTER, 40 * YR * QUARTER),
        name="low_weights",
    )(quarter, grad, master, fm, fs, sm, ss)


def state_kernel(
    idx, mine, other, master, fm, fs, sm, ss, om, of, ofs, os, oss, firsts, seconds
):
    first_half = idx[0] == 0

    def stacked(ref, b):
        halves = [ref[:, k * BLOCK : (k + 1) * BLOCK] for k in (b, b + HB)]
        return jnp.concatenate([half.astype(f32) for half in halves], axis=0)

    def scales_of(ref):
        return jnp.concatenate([ref[:, :HB], ref[:, HB:]], axis=0)

    def store(ref, b, value):
        for k, rows in ((b, slice(0, YR)), (b + HB, slice(YR, 2 * YR))):
            ref[:, k * BLOCK : (k + 1) * BLOCK] = value[rows].astype(ref.dtype)

    fscale, sscale = scales_of(fs), scales_of(ss)
    lane = lax.broadcasted_iota(jnp.int32, (2 * YR, HB), 1)
    fpeaks = jnp.zeros((2 * YR, HB), f32)
    speaks = jnp.zeros((2 * YR, HB), f32)
    for b in range(HB):
        cols = slice(b * BLOCK, (b + 1) * BLOCK)
        one, two = mine[:, cols], other[:, cols]
        gradient = jnp.concatenate(
            [jnp.where(first_half, one, two), jnp.where(first_half, two, one)], axis=0
        )
        first_old = stacked(fm, b) * fscale[:, b : b + 1]
        second_old = stacked(sm, b) * sscale[:, b : b + 1]
        first, second, updated = adam(
            gradient, stacked(master, b), first_old, second_old
        )
        store(om, b, updated)
        firsts[:, cols] = first
        seconds[:, cols] = second
        fpeak = jnp.max(jnp.abs(first), axis=1, keepdims=True)
        speak = jnp.max(second, axis=1, keepdims=True)
        fpeaks = jnp.where(lane == b, fpeak, fpeaks)
        speaks = jnp.where(lane == b, speak, speaks)
    fpeaks = fpeaks + scale_eps
    speaks = speaks + scale_eps
    for ref, peaks in ((ofs, fpeaks), (oss, speaks)):
        ref[:, :HB] = peaks[:YR]
        ref[:, HB:] = peaks[YR:]
    finverse, sinverse = 1.0 / fpeaks, 1.0 / speaks
    for b in range(HB):
        cols = slice(b * BLOCK, (b + 1) * BLOCK)
        store(of, b, firsts[:, cols] * finverse[:, b : b + 1])
        store(os, b, seconds[:, cols] * sinverse[:, b : b + 1])


def states(core, mine, other, master, fm, fs, sm, ss):
    half = pl.BlockSpec((YR, HALF), lambda i, s: (0, 0))
    whole = pl.BlockSpec((YR, D), lambda i, s: (0, 0))
    scale = pl.BlockSpec((YR, NB), lambda i, s: (0, 0))
    shape = jax.ShapeDtypeStruct
    return pl.pallas_call(
        state_kernel,
        grid_spec=pltpu.PrefetchScalarGridSpec(
            num_scalar_prefetch=1,
            grid=(1,),
            in_specs=[half, half, whole, whole, scale, whole, scale],
            out_specs=[whole, whole, scale, whole, scale],
            scratch_shapes=[pltpu.VMEM((2 * YR, HALF), f32)] * 2,
        ),
        out_shape=[
            shape((YR, D), f32),
            shape((YR, D), bf16),
            shape((YR, NB), f32),
            shape((YR, D), bf16),
            shape((YR, NB), f32),
        ],
        compiler_params=params(),
        cost_estimate=cost(60 * YR * D, 20 * YR * D),
        name="new_states",
    )(core, mine, other, master, fm, fs, sm, ss)


def place_kernel(idx, *refs):
    pieces, (weights, transposed, rows) = refs[:NX], refs[-3:]
    for shift, ref in enumerate(pieces):
        start = pl.multiple_of(lax.rem(idx[1] + NX - shift, NX) * XR, XR)
        low = ref[...].astype(f32).reshape(XR, QUARTER).astype(bf16)
        rows[pl.ds(start, XR), :] = low
    low = rows[...]
    weights[...] = low
    transposed[...] = low.T


def place(idx, pieces, before=()):
    ins, args = [], []
    for piece in pieces:
        if isinstance(piece, tuple):
            k, piece = piece
            ins.append(
                pl.BlockSpec((None, NY, YR, QUARTER), lambda j, s, k=k: (k, j, 0, 0))
            )
        else:
            ins.append(pl.BlockSpec((NY, YR, QUARTER), lambda j, s: (j, 0, 0)))
        args.append(piece)
    return pl.pallas_call(
        place_kernel,
        grid_spec=pltpu.PrefetchScalarGridSpec(
            num_scalar_prefetch=1,
            grid=(NZ,),
            in_specs=ins + [pl.BlockSpec(memory_space=pl.ANY)] * len(before),
            out_specs=[
                pl.BlockSpec((ROWS, QUARTER), lambda j, s: (0, s[0] * NZ + j)),
                pl.BlockSpec((QUARTER, ROWS), lambda j, s: (s[0] * NZ + j, 0)),
            ],
            scratch_shapes=[pltpu.VMEM((ROWS, QUARTER), bf16)],
        ),
        out_shape=[
            jax.ShapeDtypeStruct((ROWS, D), bf16),
            jax.ShapeDtypeStruct((D, ROWS), bf16),
        ],
        input_output_aliases={1 + NX: 0, 2 + NX: 1} if before else {},
        compiler_params=params(),
        cost_estimate=cost(0, 3 * ROWS * HALF * 2),
        name="place_weights",
    )(idx, *args, *before)


def shift_x(value, shift):
    return lax.ppermute(value, "x", [(i, (i + shift) % NX) for i in range(NX)])


def exchange(value, axis):
    return lax.all_to_all(value, axis, 0, 0, tiled=True)


def swap(value, axis):
    return lax.ppermute(value, axis, [(0, 1), (1, 0)])


def on_device(gv, gs, master, fm, fs, sm, ss):
    gv, gs = gv.reshape(ROWS, D), jnp.swapaxes(gs.reshape(ROWS, NB), 0, 1)
    master, fm, sm = master.reshape(YR, D), fm.reshape(YR, D), sm.reshape(YR, D)
    fs, ss = fs.reshape(YR, NB), ss.reshape(YR, NB)
    x = lax.axis_index("x").astype(jnp.int32)
    core = lax.axis_index("c").astype(jnp.int32)
    plane = lax.axis_index("zl").astype(jnp.int32)
    half = core.reshape(1)

    packed, scales = pack(1 - half, gv, gs)
    there = swap(packed, "c")
    arrived = []
    for shift in (2, 1, 3):
        target = jnp.stack([lax.rem(x + shift, NX), core])
        arrived.append(shift_x(chip_sum(target, gv, scales, there, True), shift))
    own = chip_sum(jnp.stack([x, core]), gv, scales, there, False)
    quarter = last_sum(exchange(row_sum(own, arrived), ("zl", "y")))
    low = low_weights((2 * core + plane).reshape(1), quarter, master, fm, fs, sm, ss)
    low_y = exchange(low, ("zl", "y"))

    from_z = swap(quarter, "zl")
    left = jnp.where(plane == 0, quarter, from_z)
    right = jnp.where(plane == 0, from_z, quarter)
    gradient = jnp.concatenate([left, right], axis=1)
    new = states(half, gradient, swap(gradient, "c"), master, fm, fs, sm, ss)
    low_y, new = lax.optimization_barrier((low_y, new))

    two, one, three = [shift_x(low_y, shift) for shift in (2, 1, 3)]
    other_y = swap(low_y, "c")
    rest = [swap(piece, "c") for piece in (one, two, three)]
    placed = place(jnp.stack([core, x]), [low_y, one, two, three])
    weights, transposed = place(jnp.stack([1 - core, x]), [other_y] + rest, placed)
    om, of, ofs, os, oss = [a[None] for a in new]
    return om, of, ofs, os, oss, weights[None], transposed[None]


def solution(mesh):
    fine = Mesh(
        mesh.devices.reshape(NZ, 2, NX, NY, mesh.devices.shape[-1]),
        ("zl", "c", "x", "y", "zh"),
    )
    grads = P(("zl", "c"), ("x", "y"), "zh", None, None)
    rows = P("zh", ("x", "y"), None)
    shard = P("zh", None, None)
    return jax.shard_map(
        on_device,
        mesh=fine,
        in_specs=(grads, grads, rows, rows, rows, rows, rows),
        out_specs=(rows,) * 5 + (shard, shard),
        check_vma=False,
    )
```

```python
import functools

import jax
import jax.numpy as jnp
from jax import lax
from jax.experimental import pallas as pl
from jax.experimental.pallas import tpu as pltpu
from jax.sharding import Mesh, PartitionSpec as P

D = 12288
HALF = D // 2
BLOCK = 128
NB = D // BLOCK
HB = NB // 2
ROWS = 128
NX, NY, NZ = 4, 8, 2
XR = ROWS // NX
YR = XR // NY
QUARTER = D // 4
QB = NB // 4
PAD = HALF + BLOCK
QPAD = QUARTER + BLOCK
CH = 3072
SPAN = 172.0
OFFSET = 86.0

beta_one = 0.9
beta_two = 0.95
rate = 0.02
adam_eps = 1e-08
scale_eps = 1e-06
corr_one = 1.0 - 0.9**10
corr_two = 1.0 - 0.95**10

f32 = jnp.float32
bf16 = jnp.bfloat16


def params(mib=24):
    return pltpu.CompilerParams(vmem_limit_bytes=mib * 1024 * 1024)


def cost(flops, nbytes):
    return pl.CostEstimate(flops=flops, bytes_accessed=nbytes, transcendentals=0)


def encode(value, factor):
    size = jnp.exp(jnp.abs(value) * factor - OFFSET)
    return jnp.where(value < 0, -size, size)


def decode(code, step):
    size = (jnp.log(jnp.abs(code)) + OFFSET) * step
    return jnp.where(code < 0, -size, size)


def scale_of(peak):
    return jnp.maximum(peak * (1.0 + 2.0**-7), 1e-30).astype(bf16)


def pack_kernel(idx, v0, v1, v2, v3, scales, out, rows):
    rows[...] = scales[...].astype(f32).T
    pad = jnp.zeros((XR, BLOCK - HB), bf16)
    for k, values in enumerate((v0, v1, v2, v3)):
        start = pl.multiple_of(idx[1 + k] * XR, XR)
        block = rows[pl.ds(start, XR), :]
        chosen = jnp.where(idx[0] == 0, block[:, :HB], block[:, HB:])
        out[k, :, :HALF] = values[...]
        out[k, :, HALF : HALF + HB] = chosen.astype(bf16)
        out[k, :, HALF + HB :] = pad


def pack(idx, values, scales, name):
    values = in_hbm(values)
    rows = [
        pl.BlockSpec((XR, HALF), lambda i, s, k=k: (s[1 + k], s[0])) for k in range(NX)
    ]
    return pl.pallas_call(
        pack_kernel,
        grid_spec=pltpu.PrefetchScalarGridSpec(
            num_scalar_prefetch=1,
            grid=(1,),
            in_specs=rows + [pl.BlockSpec((NB, ROWS), lambda i, s: (0, 0))],
            out_specs=pl.BlockSpec((NX, XR, PAD), lambda i, s: (0, 0, 0)),
            scratch_shapes=[pltpu.VMEM((ROWS, NB), f32)],
        ),
        out_shape=jax.ShapeDtypeStruct((NX, XR, PAD), bf16),
        compiler_params=params(),
        cost_estimate=cost(0, 4 * ROWS * HALF * 2),
        name=name,
    )(idx, *([values] * NX), in_hbm(scales))


def in_hbm(value):
    return pltpu.with_memory_space_constraint(value, pltpu.HBM)


def add_cores(values, scales, there, there_scales, totals):
    mine = scales[...].astype(f32)
    theirs = there_scales[...].astype(f32)
    peak = jnp.zeros((XR, BLOCK), f32)
    for b in range(HB):
        cols = slice(b * BLOCK, (b + 1) * BLOCK)
        total = values[:, cols].astype(f32) * mine[:, b : b + 1]
        total = total + there[:, cols].astype(f32) * theirs[:, b : b + 1]
        totals[:, cols] = total
        peak = jnp.maximum(peak, jnp.abs(total))
    return peak


def code_kernel(values, scales, there, there_scales, out, totals):
    scale = scale_of(add_cores(values, scales, there, there_scales, totals))
    out[:, HALF:] = scale
    factor = SPAN / scale.astype(f32)
    for b in range(HB):
        cols = slice(b * BLOCK, (b + 1) * BLOCK)
        out[:, cols] = encode(totals[:, cols], factor).astype(bf16)


def own_kernel(values, scales, there, there_scales, out):
    add_cores(values, scales, there, there_scales, out)


def chip_sum(k, own, there, coded):
    if coded:
        kernel, width, kind, name = code_kernel, PAD, bf16, "coded_chip_sum"
        scratch = [pltpu.VMEM((XR, HALF), f32)]
    else:
        kernel, width, kind, name = own_kernel, HALF, f32, "own_chip_sum"
        scratch = []
    value = pl.BlockSpec((None, XR, HALF), lambda i: (k, 0, 0))
    scale = pl.BlockSpec((None, XR, BLOCK), lambda i: (k, 0, HB))
    return pl.pallas_call(
        kernel,
        grid=(1,),
        in_specs=[value, scale, value, scale],
        out_specs=pl.BlockSpec((XR, width), lambda i: (0, 0)),
        scratch_shapes=scratch,
        out_shape=jax.ShapeDtypeStruct((XR, width), kind),
        compiler_params=params(),
        cost_estimate=cost(20 * XR * HALF, 6 * XR * HALF),
        name=name,
    )(own, own, there, there)


def row_kernel(own, c1, s1, c2, s2, c3, s3, out, totals):
    coded = [
        (ref, scale[...].astype(f32) * (1.0 / SPAN))
        for ref, scale in ((c1, s1), (c2, s2), (c3, s3))
    ]
    peak = jnp.zeros((XR, BLOCK), f32)
    for b in range(HB):
        cols = slice(b * BLOCK, (b + 1) * BLOCK)
        total = own[:, cols]
        for ref, step in coded:
            total = total + decode(ref[:, cols].astype(f32), step)
        totals[:, cols] = total
        peak = jnp.maximum(peak, jnp.abs(total))
    scale = scale_of(peak).astype(f32)
    for z in range(NZ):
        planes = slice(z * NY, (z + 1) * NY)
        out[planes, :, QUARTER:] = scale.reshape(NY, YR, BLOCK).astype(bf16)
    factor = SPAN / scale
    for b in range(HB):
        cols = slice(b * BLOCK, (b + 1) * BLOCK)
        z, inner = b // QB, slice(b % QB * BLOCK, (b % QB + 1) * BLOCK)
        code = encode(totals[:, cols], factor)
        out[z * NY : (z + 1) * NY, :, inner] = code.reshape(NY, YR, BLOCK).astype(bf16)


def row_sum(own, arrived):
    ins = [pl.BlockSpec((XR, HALF), lambda i: (0, 0))]
    args = [own]
    for a in arrived:
        ins += [
            pl.BlockSpec((XR, HALF), lambda i: (0, 0)),
            pl.BlockSpec((XR, BLOCK), lambda i: (0, HB)),
        ]
        args += [a, a]
    return pl.pallas_call(
        row_kernel,
        grid=(1,),
        in_specs=ins,
        out_specs=pl.BlockSpec((NZ * NY, YR, QPAD), lambda i: (0, 0, 0)),
        scratch_shapes=[pltpu.VMEM((XR, HALF), f32)],
        out_shape=jax.ShapeDtypeStruct((NZ * NY, YR, QPAD), bf16),
        compiler_params=params(),
        cost_estimate=cost(60 * XR * HALF, 12 * XR * HALF),
        name="sum_over_x",
    )(*args)


def adam(gradient, master, first_old, second_old):
    first = beta_one * first_old + (1.0 - beta_one) * gradient
    second = beta_two * second_old + (1.0 - beta_two) * gradient * gradient
    direction = first / corr_one / (jnp.sqrt(second / corr_two) + adam_eps)
    return first, second, master - rate * direction


def low_kernel(idx, codes, steps, master, fm, fs, sm, ss, grad_out, low_out):
    def chosen(ref):
        scales = ref[...]
        parts = [scales[:, k * QB : (k + 1) * QB] for k in range(4)]
        low = jnp.where(idx[0] == 0, parts[0], parts[1])
        high = jnp.where(idx[0] == 2, parts[2], parts[3])
        return jnp.where(idx[0] < 2, low, high)

    parts = NZ * NY * YR
    step = steps[...].astype(f32).reshape(parts, BLOCK) * (1.0 / SPAN)
    fscale, sscale = chosen(fs), chosen(ss)
    for b in range(QB):
        cols = slice(b * BLOCK, (b + 1) * BLOCK)
        code = codes[:, :, cols].astype(f32).reshape(parts, BLOCK)
        term = decode(code, step).reshape(NZ * NY, YR, BLOCK)
        gradient = jnp.sum(term, axis=0)
        grad_out[:, cols] = gradient
        first_old = fm[:, cols].astype(f32) * fscale[:, b : b + 1]
        second_old = sm[:, cols].astype(f32) * sscale[:, b : b + 1]
        _, _, updated = adam(gradient, master[:, cols], first_old, second_old)
        low = updated.astype(bf16)
        for i in range(NZ * NY):
            low_out[i, :, cols] = low


def low_weights(quarter, codes, master, fm, fs, sm, ss):
    part = pl.BlockSpec((YR, QUARTER), lambda i, s: (0, s[0]))
    scale = pl.BlockSpec((YR, NB), lambda i, s: (0, 0))
    return pl.pallas_call(
        low_kernel,
        grid_spec=pltpu.PrefetchScalarGridSpec(
            num_scalar_prefetch=1,
            grid=(1,),
            in_specs=[
                pl.BlockSpec((NZ * NY, YR, QUARTER), lambda i, s: (0, 0, 0)),
                pl.BlockSpec((NZ * NY, YR, BLOCK), lambda i, s: (0, 0, QB)),
                part,
                part,
                scale,
                part,
                scale,
            ],
            out_specs=[
                pl.BlockSpec((YR, QUARTER), lambda i, s: (0, 0)),
                pl.BlockSpec((NZ * NY, YR, QUARTER), lambda i, s: (0, 0, 0)),
            ],
        ),
        out_shape=[
            jax.ShapeDtypeStruct((YR, QUARTER), f32),
            jax.ShapeDtypeStruct((NZ * NY, YR, QUARTER), bf16),
        ],
        compiler_params=params(),
        cost_estimate=cost(30 * XR * HALF, 8 * XR * HALF),
        name="sum_and_low_weights",
    )(quarter, codes, codes, master, fm, fs, sm, ss)


def state_kernel(
    idx, mine, other, master, fm, fs, sm, ss, om, of, ofs, os, oss, firsts, seconds
):
    first_half = idx[0] == 0

    def stacked(ref, b):
        halves = [ref[:, k * BLOCK : (k + 1) * BLOCK] for k in (b, b + HB)]
        return jnp.concatenate([half.astype(f32) for half in halves], axis=0)

    def scales_of(ref):
        return jnp.concatenate([ref[:, :HB], ref[:, HB:]], axis=0)

    def store(ref, b, value):
        for k, rows in ((b, slice(0, YR)), (b + HB, slice(YR, 2 * YR))):
            ref[:, k * BLOCK : (k + 1) * BLOCK] = value[rows].astype(ref.dtype)

    fscale, sscale = scales_of(fs), scales_of(ss)
    lane = lax.broadcasted_iota(jnp.int32, (2 * YR, HB), 1)
    fpeaks = jnp.zeros((2 * YR, HB), f32)
    speaks = jnp.zeros((2 * YR, HB), f32)
    for b in range(HB):
        cols = slice(b * BLOCK, (b + 1) * BLOCK)
        one, two = mine[:, cols], other[:, cols]
        gradient = jnp.concatenate(
            [jnp.where(first_half, one, two), jnp.where(first_half, two, one)], axis=0
        )
        first_old = stacked(fm, b) * fscale[:, b : b + 1]
        second_old = stacked(sm, b) * sscale[:, b : b + 1]
        first, second, updated = adam(
            gradient, stacked(master, b), first_old, second_old
        )
        store(om, b, updated)
        firsts[:, cols] = first
        seconds[:, cols] = second
        fpeak = jnp.max(jnp.abs(first), axis=1, keepdims=True)
        speak = jnp.max(second, axis=1, keepdims=True)
        fpeaks = jnp.where(lane == b, fpeak, fpeaks)
        speaks = jnp.where(lane == b, speak, speaks)
    fpeaks = fpeaks + scale_eps
    speaks = speaks + scale_eps
    for ref, peaks in ((ofs, fpeaks), (oss, speaks)):
        ref[:, :HB] = peaks[:YR]
        ref[:, HB:] = peaks[YR:]
    finverse, sinverse = 1.0 / fpeaks, 1.0 / speaks
    for b in range(HB):
        cols = slice(b * BLOCK, (b + 1) * BLOCK)
        store(of, b, firsts[:, cols] * finverse[:, b : b + 1])
        store(os, b, seconds[:, cols] * sinverse[:, b : b + 1])


def states(core, mine, other, master, fm, fs, sm, ss):
    half = pl.BlockSpec((YR, HALF), lambda i, s: (0, 0))
    whole = pl.BlockSpec((YR, D), lambda i, s: (0, 0))
    scale = pl.BlockSpec((YR, NB), lambda i, s: (0, 0))
    shape = jax.ShapeDtypeStruct
    return pl.pallas_call(
        state_kernel,
        grid_spec=pltpu.PrefetchScalarGridSpec(
            num_scalar_prefetch=1,
            grid=(1,),
            in_specs=[half, half, whole, whole, scale, whole, scale],
            out_specs=[whole, whole, scale, whole, scale],
            scratch_shapes=[pltpu.VMEM((2 * YR, HALF), f32)] * 2,
        ),
        out_shape=[
            shape((YR, D), f32),
            shape((YR, D), bf16),
            shape((YR, NB), f32),
            shape((YR, D), bf16),
            shape((YR, NB), f32),
        ],
        compiler_params=params(),
        cost_estimate=cost(YR * D, YR * D),
        name="new_states",
    )(core, mine, other, master, fm, fs, sm, ss)


def spread_kernel(low, out):
    for z in range(NZ):
        cols = slice(z * QUARTER, (z + 1) * QUARTER)
        rows = low[z * NY : (z + 1) * NY].astype(f32).reshape(XR, QUARTER)
        for k in range(NX):
            out[k, :, cols] = rows.astype(bf16)


def spread(low):
    return pl.pallas_call(
        spread_kernel,
        grid=(1,),
        in_specs=[pl.BlockSpec((NZ * NY, YR, QUARTER), lambda i: (0, 0, 0))],
        out_specs=pl.BlockSpec((NX, XR, HALF), lambda i: (0, 0, 0)),
        out_shape=jax.ShapeDtypeStruct((NX, XR, HALF), bf16),
        compiler_params=params(),
        cost_estimate=cost(0, 10 * XR * HALF),
        name="spread_rows",
    )(low)


def place_kernel(idx, piece, *refs):
    weights, transposed = refs[-2:]
    low = piece[...].reshape(ROWS, CH)
    weights[...] = low
    transposed[...] = low.T


def place(half, piece, before=()):
    steps = HALF // CH
    return pl.pallas_call(
        place_kernel,
        grid_spec=pltpu.PrefetchScalarGridSpec(
            num_scalar_prefetch=1,
            grid=(steps,),
            in_specs=[pl.BlockSpec((NX, XR, CH), lambda j, s: (0, 0, j))]
            + [pl.BlockSpec(memory_space=pl.ANY)] * len(before),
            out_specs=[
                pl.BlockSpec((ROWS, CH), lambda j, s: (0, s[0] * steps + j)),
                pl.BlockSpec((CH, ROWS), lambda j, s: (s[0] * steps + j, 0)),
            ],
        ),
        out_shape=[
            jax.ShapeDtypeStruct((ROWS, D), bf16),
            jax.ShapeDtypeStruct((D, ROWS), bf16),
        ],
        input_output_aliases={2: 0, 3: 1} if before else {},
        compiler_params=params(),
        cost_estimate=cost(0, 3 * ROWS * HALF * 2),
        name="place_weights",
    )(half, piece, *before)


def shift_x(value, shift):
    return lax.ppermute(value, "x", [(i, (i + shift) % NX) for i in range(NX)])


def exchange(value, axis):
    return lax.all_to_all(value, axis, 0, 0, tiled=True)


def swap(value, axis):
    return lax.ppermute(value, axis, [(0, 1), (1, 0)])


def on_device(gv, gs, master, fm, fs, sm, ss):
    gv, gs = gv.reshape(ROWS, D), jnp.swapaxes(gs.reshape(ROWS, NB), 0, 1)
    master, fm, sm = master.reshape(YR, D), fm.reshape(YR, D), sm.reshape(YR, D)
    fs, ss = fs.reshape(YR, NB), ss.reshape(YR, NB)
    x = lax.axis_index("x").astype(jnp.int32)
    core = lax.axis_index("c").astype(jnp.int32)
    plane = lax.axis_index("zl").astype(jnp.int32)
    half = core.reshape(1)

    def blocks(*shifts):
        return [lax.rem(x + shift, NX) for shift in shifts]

    order = blocks(2, 1, 3, 0)
    packed = pack(jnp.stack([1 - core] + order), gv, gs, "pack_theirs")
    mine = pack(jnp.stack([core] + order), gv, gs, "pack_mine")
    there = swap(packed, "c")
    arrived = [
        shift_x(chip_sum(k, mine, there, True), shift)
        for k, shift in enumerate((2, 1, 3))
    ]
    own = chip_sum(3, mine, there, False)
    codes = exchange(row_sum(own, arrived), ("zl", "y"))
    quarter, low = low_weights(
        (2 * core + plane).reshape(1), codes, master, fm, fs, sm, ss
    )
    low_y = exchange(low, ("zl", "y"))

    from_z = swap(quarter, "zl")
    left = jnp.where(plane == 0, quarter, from_z)
    right = jnp.where(plane == 0, from_z, quarter)
    gradient = jnp.concatenate([left, right], axis=1)
    low_y, gradient = lax.optimization_barrier((low_y, gradient))
    other_gradient = swap(gradient, "c")
    new = states(half, gradient, other_gradient, master, fm, fs, sm, ss)

    near = exchange(spread(low_y), "x")
    near, new = lax.optimization_barrier((near, new))
    far = swap(near, "c")
    weights, transposed = place(1 - half, far, place(half, near))
    om, of, ofs, os, oss = [a[None] for a in new]
    return om, of, ofs, os, oss, weights[None], transposed[None]


def solution(mesh):
    fine = Mesh(
        mesh.devices.reshape(NZ, 2, NX, NY, mesh.devices.shape[-1]),
        ("zl", "c", "x", "y", "zh"),
    )
    grads = P(("zl", "c"), ("x", "y"), "zh", None, None)
    rows = P("zh", ("x", "y"), None)
    shard = P("zh", None, None)
    return jax.shard_map(
        on_device,
        mesh=fine,
        in_specs=(grads, grads, rows, rows, rows, rows, rows),
        out_specs=(rows,) * 5 + (shard, shard),
        check_vma=False,
    )
```

```python
import functools

import jax
import jax.numpy as jnp
from jax import lax
from jax.experimental import pallas as pl
from jax.experimental.pallas import tpu as pltpu
from jax.sharding import Mesh, PartitionSpec as P

D = 12288
HALF = D // 2
OLD_BYTES = 24 * 1024 * 1024
BLOCK = 128
NB = D // BLOCK
HB = NB // 2
ROWS = 128
NX, NY, NZ = 4, 8, 2
XR = ROWS // NX
YR = XR // NY
QUARTER = D // 4
QB = NB // 4
PAD = HALF + BLOCK
QPAD = QUARTER + BLOCK
CH = 3072
SPAN = 172.0
OFFSET = 86.0

beta_one = 0.9
beta_two = 0.95
rate = 0.02
adam_eps = 1e-08
scale_eps = 1e-06
corr_one = 1.0 - 0.9**10
corr_two = 1.0 - 0.95**10

f32 = jnp.float32
bf16 = jnp.bfloat16


def params(mib=24):
    return pltpu.CompilerParams(vmem_limit_bytes=mib * 1024 * 1024)


def cost(flops, nbytes):
    return pl.CostEstimate(flops=flops, bytes_accessed=nbytes, transcendentals=0)


def encode(value, factor):
    size = jnp.exp(jnp.abs(value) * factor - OFFSET)
    return jnp.where(value < 0, -size, size)


def decode(code, step):
    size = (jnp.log(jnp.abs(code)) + OFFSET) * step
    return jnp.where(code < 0, -size, size)


def scale_of(peak):
    return jnp.maximum(peak * (1.0 + 2.0**-7), 1e-30).astype(bf16)


def pack_kernel(idx, v0, v1, v2, v3, scales, out, rows):
    rows[...] = scales[...].astype(f32).T
    pad = jnp.zeros((XR, BLOCK - HB), bf16)
    for k, values in enumerate((v0, v1, v2, v3)):
        start = pl.multiple_of(idx[1 + k] * XR, XR)
        block = rows[pl.ds(start, XR), :]
        chosen = jnp.where(idx[0] == 0, block[:, :HB], block[:, HB:])
        out[k, :, :HALF] = values[...]
        out[k, :, HALF : HALF + HB] = chosen.astype(bf16)
        out[k, :, HALF + HB :] = pad


def pack(idx, values, scales, name):
    values = in_hbm(values)
    rows = [
        pl.BlockSpec((XR, HALF), lambda i, s, k=k: (s[1 + k], s[0])) for k in range(NX)
    ]
    return pl.pallas_call(
        pack_kernel,
        grid_spec=pltpu.PrefetchScalarGridSpec(
            num_scalar_prefetch=1,
            grid=(1,),
            in_specs=rows + [pl.BlockSpec((NB, ROWS), lambda i, s: (0, 0))],
            out_specs=pl.BlockSpec((NX, XR, PAD), lambda i, s: (0, 0, 0)),
            scratch_shapes=[pltpu.VMEM((ROWS, NB), f32)],
        ),
        out_shape=jax.ShapeDtypeStruct((NX, XR, PAD), bf16),
        compiler_params=params(),
        cost_estimate=cost(0, 4 * ROWS * HALF * 2),
        name=name,
    )(idx, *([values] * NX), in_hbm(scales))


def in_hbm(value):
    return pltpu.with_memory_space_constraint(value, pltpu.HBM)


def add_cores(values, scales, there, there_scales, totals):
    mine = scales[...].astype(f32)
    theirs = there_scales[...].astype(f32)
    peak = jnp.zeros((XR, BLOCK), f32)
    for b in range(HB):
        cols = slice(b * BLOCK, (b + 1) * BLOCK)
        total = values[:, cols].astype(f32) * mine[:, b : b + 1]
        total = total + there[:, cols].astype(f32) * theirs[:, b : b + 1]
        totals[:, cols] = total
        peak = jnp.maximum(peak, jnp.abs(total))
    return peak


def code_kernel(values, scales, there, there_scales, out, totals):
    scale = scale_of(add_cores(values, scales, there, there_scales, totals))
    out[:, HALF:] = scale
    factor = SPAN / scale.astype(f32)
    for b in range(HB):
        cols = slice(b * BLOCK, (b + 1) * BLOCK)
        out[:, cols] = encode(totals[:, cols], factor).astype(bf16)


def own_kernel(values, scales, there, there_scales, out):
    add_cores(values, scales, there, there_scales, out)


def chip_sum(k, own, there, coded):
    if coded:
        kernel, width, kind, name = code_kernel, PAD, bf16, "coded_chip_sum"
        scratch = [pltpu.VMEM((XR, HALF), f32)]
    else:
        kernel, width, kind, name = own_kernel, HALF, f32, "own_chip_sum"
        scratch = []
    value = pl.BlockSpec((None, XR, HALF), lambda i: (k, 0, 0))
    scale = pl.BlockSpec((None, XR, BLOCK), lambda i: (k, 0, HB))
    return pl.pallas_call(
        kernel,
        grid=(1,),
        in_specs=[value, scale, value, scale],
        out_specs=pl.BlockSpec((XR, width), lambda i: (0, 0)),
        scratch_shapes=scratch,
        out_shape=jax.ShapeDtypeStruct((XR, width), kind),
        compiler_params=params(),
        cost_estimate=cost(20 * XR * HALF, 6 * XR * HALF),
        name=name,
    )(own, own, there, there)


def row_kernel(own, c1, s1, c2, s2, c3, s3, out, totals):
    coded = [
        (ref, scale[...].astype(f32) * (1.0 / SPAN))
        for ref, scale in ((c1, s1), (c2, s2), (c3, s3))
    ]
    peak = jnp.zeros((XR, BLOCK), f32)
    for b in range(HB):
        cols = slice(b * BLOCK, (b + 1) * BLOCK)
        total = own[:, cols]
        for ref, step in coded:
            total = total + decode(ref[:, cols].astype(f32), step)
        totals[:, cols] = total
        peak = jnp.maximum(peak, jnp.abs(total))
    scale = scale_of(peak).astype(f32)
    for z in range(NZ):
        planes = slice(z * NY, (z + 1) * NY)
        out[planes, :, QUARTER:] = scale.reshape(NY, YR, BLOCK).astype(bf16)
    factor = SPAN / scale
    for b in range(HB):
        cols = slice(b * BLOCK, (b + 1) * BLOCK)
        z, inner = b // QB, slice(b % QB * BLOCK, (b % QB + 1) * BLOCK)
        code = encode(totals[:, cols], factor)
        out[z * NY : (z + 1) * NY, :, inner] = code.reshape(NY, YR, BLOCK).astype(bf16)


def row_sum(own, arrived):
    ins = [pl.BlockSpec((XR, HALF), lambda i: (0, 0))]
    args = [own]
    for a in arrived:
        ins += [
            pl.BlockSpec((XR, HALF), lambda i: (0, 0)),
            pl.BlockSpec((XR, BLOCK), lambda i: (0, HB)),
        ]
        args += [a, a]
    return pl.pallas_call(
        row_kernel,
        grid=(1,),
        in_specs=ins,
        out_specs=pl.BlockSpec((NZ * NY, YR, QPAD), lambda i: (0, 0, 0)),
        scratch_shapes=[pltpu.VMEM((XR, HALF), f32)],
        out_shape=jax.ShapeDtypeStruct((NZ * NY, YR, QPAD), bf16),
        compiler_params=params(),
        cost_estimate=cost(60 * XR * HALF, 12 * XR * HALF),
        name="sum_over_x",
    )(*args)


def adam(gradient, master, first_old, second_old):
    first = beta_one * first_old + (1.0 - beta_one) * gradient
    second = beta_two * second_old + (1.0 - beta_two) * gradient * gradient
    direction = first / corr_one / (jnp.sqrt(second / corr_two) + adam_eps)
    return first, second, master - rate * direction


def low_kernel(idx, codes, steps, master, fm, fs, sm, ss, grad_out, low_out):
    def chosen(ref):
        scales = ref[...]
        parts = [scales[:, k * QB : (k + 1) * QB] for k in range(4)]
        low = jnp.where(idx[0] == 0, parts[0], parts[1])
        high = jnp.where(idx[0] == 2, parts[2], parts[3])
        return jnp.where(idx[0] < 2, low, high)

    parts = NZ * NY * YR
    step = steps[...].astype(f32).reshape(parts, BLOCK) * (1.0 / SPAN)
    fscale, sscale = chosen(fs), chosen(ss)
    for b in range(QB):
        cols = slice(b * BLOCK, (b + 1) * BLOCK)
        code = codes[:, :, cols].astype(f32).reshape(parts, BLOCK)
        term = decode(code, step).reshape(NZ * NY, YR, BLOCK)
        gradient = jnp.sum(term, axis=0)
        grad_out[:, cols] = gradient
        first_old = fm[:, cols].astype(f32) * fscale[:, b : b + 1]
        second_old = sm[:, cols].astype(f32) * sscale[:, b : b + 1]
        _, _, updated = adam(gradient, master[:, cols], first_old, second_old)
        low = updated.astype(bf16)
        for i in range(NZ * NY):
            low_out[i, :, cols] = low


def low_weights(quarter, codes, master, fm, fs, sm, ss):
    part = pl.BlockSpec((YR, QUARTER), lambda i, s: (0, s[0]))
    scale = pl.BlockSpec((YR, NB), lambda i, s: (0, 0))
    return pl.pallas_call(
        low_kernel,
        grid_spec=pltpu.PrefetchScalarGridSpec(
            num_scalar_prefetch=1,
            grid=(1,),
            in_specs=[
                pl.BlockSpec((NZ * NY, YR, QUARTER), lambda i, s: (0, 0, 0)),
                pl.BlockSpec((NZ * NY, YR, BLOCK), lambda i, s: (0, 0, QB)),
                part,
                part,
                scale,
                part,
                scale,
            ],
            out_specs=[
                pl.BlockSpec((YR, QUARTER), lambda i, s: (0, 0)),
                pl.BlockSpec((NZ * NY, YR, QUARTER), lambda i, s: (0, 0, 0)),
            ],
        ),
        out_shape=[
            jax.ShapeDtypeStruct((YR, QUARTER), f32),
            jax.ShapeDtypeStruct((NZ * NY, YR, QUARTER), bf16),
        ],
        compiler_params=params(),
        cost_estimate=cost(30 * XR * HALF, 8 * XR * HALF),
        name="sum_and_low_weights",
    )(quarter, codes, codes, master, fm, fs, sm, ss)


def old_kernel(fm, fs, sm, ss, of, os):
    for moment, scales, out in ((fm, fs, of), (sm, ss, os)):
        scale = jnp.concatenate([scales[:, :HB], scales[:, HB:]], axis=0)
        for b in range(HB):
            cols = slice(b * BLOCK, (b + 1) * BLOCK)
            halves = [moment[:, k * BLOCK : (k + 1) * BLOCK] for k in (b, b + HB)]
            both = jnp.concatenate([half.astype(f32) for half in halves], axis=0)
            out[:, cols] = both * scale[:, b : b + 1]


def old_moments(fm, fs, sm, ss):
    whole = pl.BlockSpec((YR, D), lambda i: (0, 0))
    scale = pl.BlockSpec((YR, NB), lambda i: (0, 0))
    stacked = pl.BlockSpec((2 * YR, HALF), lambda i: (0, 0))
    return pl.pallas_call(
        old_kernel,
        grid=(1,),
        in_specs=[whole, scale, whole, scale],
        out_specs=[stacked, stacked],
        out_shape=[jax.ShapeDtypeStruct((2 * YR, HALF), f32)] * 2,
        compiler_params=params(),
        cost_estimate=cost(2 * YR * D, OLD_BYTES),
        name="old_moments",
    )(fm, fs, sm, ss)


def state_kernel(
    idx, mine, other, master, fold, sold, om, of, ofs, os, oss, firsts, seconds
):
    first_half = idx[0] == 0

    def stacked(ref, b):
        halves = [ref[:, k * BLOCK : (k + 1) * BLOCK] for k in (b, b + HB)]
        return jnp.concatenate([half.astype(f32) for half in halves], axis=0)

    def store(ref, b, value):
        for k, rows in ((b, slice(0, YR)), (b + HB, slice(YR, 2 * YR))):
            ref[:, k * BLOCK : (k + 1) * BLOCK] = value[rows].astype(ref.dtype)

    lane = lax.broadcasted_iota(jnp.int32, (2 * YR, HB), 1)
    fpeaks = jnp.zeros((2 * YR, HB), f32)
    speaks = jnp.zeros((2 * YR, HB), f32)
    for b in range(HB):
        cols = slice(b * BLOCK, (b + 1) * BLOCK)
        one, two = mine[:, cols], other[:, cols]
        gradient = jnp.concatenate(
            [jnp.where(first_half, one, two), jnp.where(first_half, two, one)], axis=0
        )
        first, second, updated = adam(
            gradient, stacked(master, b), fold[:, cols], sold[:, cols]
        )
        store(om, b, updated)
        firsts[:, cols] = first
        seconds[:, cols] = second
        fpeak = jnp.max(jnp.abs(first), axis=1, keepdims=True)
        speak = jnp.max(second, axis=1, keepdims=True)
        fpeaks = jnp.where(lane == b, fpeak, fpeaks)
        speaks = jnp.where(lane == b, speak, speaks)
    fpeaks = fpeaks + scale_eps
    speaks = speaks + scale_eps
    for ref, peaks in ((ofs, fpeaks), (oss, speaks)):
        ref[:, :HB] = peaks[:YR]
        ref[:, HB:] = peaks[YR:]
    finverse, sinverse = 1.0 / fpeaks, 1.0 / speaks
    for b in range(HB):
        cols = slice(b * BLOCK, (b + 1) * BLOCK)
        store(of, b, firsts[:, cols] * finverse[:, b : b + 1])
        store(os, b, seconds[:, cols] * sinverse[:, b : b + 1])


def states(core, mine, other, master, fold, sold):
    half = pl.BlockSpec((YR, HALF), lambda i, s: (0, 0))
    whole = pl.BlockSpec((YR, D), lambda i, s: (0, 0))
    scale = pl.BlockSpec((YR, NB), lambda i, s: (0, 0))
    stacked = pl.BlockSpec((2 * YR, HALF), lambda i, s: (0, 0))
    shape = jax.ShapeDtypeStruct
    return pl.pallas_call(
        state_kernel,
        grid_spec=pltpu.PrefetchScalarGridSpec(
            num_scalar_prefetch=1,
            grid=(1,),
            in_specs=[half, half, whole, stacked, stacked],
            out_specs=[whole, whole, scale, whole, scale],
            scratch_shapes=[pltpu.VMEM((2 * YR, HALF), f32)] * 2,
        ),
        out_shape=[
            shape((YR, D), f32),
            shape((YR, D), bf16),
            shape((YR, NB), f32),
            shape((YR, D), bf16),
            shape((YR, NB), f32),
        ],
        compiler_params=params(),
        cost_estimate=cost(YR * D, YR * D),
        name="new_states",
    )(core, mine, other, master, fold, sold)


def spread_kernel(low, out):
    for z in range(NZ):
        cols = slice(z * QUARTER, (z + 1) * QUARTER)
        rows = low[z * NY : (z + 1) * NY].astype(f32).reshape(XR, QUARTER)
        for k in range(NX):
            out[k, :, cols] = rows.astype(bf16)


def spread(low):
    return pl.pallas_call(
        spread_kernel,
        grid=(1,),
        in_specs=[pl.BlockSpec((NZ * NY, YR, QUARTER), lambda i: (0, 0, 0))],
        out_specs=pl.BlockSpec((NX, XR, HALF), lambda i: (0, 0, 0)),
        out_shape=jax.ShapeDtypeStruct((NX, XR, HALF), bf16),
        compiler_params=params(),
        cost_estimate=cost(0, 10 * XR * HALF),
        name="spread_rows",
    )(low)


def place_kernel(idx, piece, *refs):
    weights, transposed = refs[-2:]
    low = piece[...].reshape(ROWS, CH)
    weights[...] = low
    transposed[...] = low.T


def place(half, piece, before=()):
    steps = HALF // CH
    return pl.pallas_call(
        place_kernel,
        grid_spec=pltpu.PrefetchScalarGridSpec(
            num_scalar_prefetch=1,
            grid=(steps,),
            in_specs=[pl.BlockSpec((NX, XR, CH), lambda j, s: (0, 0, j))]
            + [pl.BlockSpec(memory_space=pl.ANY)] * len(before),
            out_specs=[
                pl.BlockSpec((ROWS, CH), lambda j, s: (0, s[0] * steps + j)),
                pl.BlockSpec((CH, ROWS), lambda j, s: (s[0] * steps + j, 0)),
            ],
        ),
        out_shape=[
            jax.ShapeDtypeStruct((ROWS, D), bf16),
            jax.ShapeDtypeStruct((D, ROWS), bf16),
        ],
        input_output_aliases={2: 0, 3: 1} if before else {},
        compiler_params=params(),
        cost_estimate=cost(0, 3 * ROWS * HALF * 2),
        name="place_weights",
    )(half, piece, *before)


def shift_x(value, shift):
    return lax.ppermute(value, "x", [(i, (i + shift) % NX) for i in range(NX)])


def exchange(value, axis):
    return lax.all_to_all(value, axis, 0, 0, tiled=True)


def swap(value, axis):
    return lax.ppermute(value, axis, [(0, 1), (1, 0)])


def on_device(gv, gs, master, fm, fs, sm, ss):
    gv, gs = gv.reshape(ROWS, D), jnp.swapaxes(gs.reshape(ROWS, NB), 0, 1)
    master, fm, sm = master.reshape(YR, D), fm.reshape(YR, D), sm.reshape(YR, D)
    fs, ss = fs.reshape(YR, NB), ss.reshape(YR, NB)
    x = lax.axis_index("x").astype(jnp.int32)
    core = lax.axis_index("c").astype(jnp.int32)
    plane = lax.axis_index("zl").astype(jnp.int32)
    half = core.reshape(1)

    def blocks(*shifts):
        return [lax.rem(x + shift, NX) for shift in shifts]

    order = blocks(2, 1, 3, 0)
    packed = pack(jnp.stack([1 - core] + order), gv, gs, "pack_theirs")
    mine = pack(jnp.stack([core] + order), gv, gs, "pack_mine")
    there = swap(packed, "c")
    arrived = [
        shift_x(chip_sum(k, mine, there, True), shift)
        for k, shift in enumerate((2, 1, 3))
    ]
    own = chip_sum(3, mine, there, False)
    codes = exchange(row_sum(own, arrived), ("zl", "y"))
    quarter, low = low_weights(
        (2 * core + plane).reshape(1), codes, master, fm, fs, sm, ss
    )
    low_y = exchange(low, ("zl", "y"))
    quarter, fm, fs, sm, ss = lax.optimization_barrier((quarter, fm, fs, sm, ss))
    fold, sold = old_moments(fm, fs, sm, ss)

    from_z = swap(quarter, "zl")
    left = jnp.where(plane == 0, quarter, from_z)
    right = jnp.where(plane == 0, from_z, quarter)
    gradient = jnp.concatenate([left, right], axis=1)
    other_gradient = swap(gradient, "c")
    new = states(half, gradient, other_gradient, master, fold, sold)

    near = exchange(spread(low_y), "x")
    near, new = lax.optimization_barrier((near, new))
    far = swap(near, "c")
    weights, transposed = place(1 - half, far, place(half, near))
    om, of, ofs, os, oss = [a[None] for a in new]
    return om, of, ofs, os, oss, weights[None], transposed[None]


def solution(mesh):
    fine = Mesh(
        mesh.devices.reshape(NZ, 2, NX, NY, mesh.devices.shape[-1]),
        ("zl", "c", "x", "y", "zh"),
    )
    grads = P(("zl", "c"), ("x", "y"), "zh", None, None)
    rows = P("zh", ("x", "y"), None)
    shard = P("zh", None, None)
    return jax.shard_map(
        on_device,
        mesh=fine,
        in_specs=(grads, grads, rows, rows, rows, rows, rows),
        out_specs=(rows,) * 5 + (shard, shard),
        check_vma=False,
    )
```

```python
import functools

import jax
import jax.numpy as jnp
from jax import lax
from jax.experimental import pallas as pl
from jax.experimental.pallas import tpu as pltpu
from jax.sharding import Mesh, PartitionSpec as P

D = 12288
HALF = D // 2
OLD_BYTES = 24 * 1024 * 1024
BLOCK = 128
NB = D // BLOCK
HB = NB // 2
ROWS = 128
NX, NY, NZ = 4, 8, 2
XR = ROWS // NX
YR = XR // NY
QUARTER = D // 4
QB = NB // 4
PAD = HALF + BLOCK
QPAD = QUARTER + BLOCK
CH = 3072
SPAN = 172.0
OFFSET = 86.0

beta_one = 0.9
beta_two = 0.95
rate = 0.02
adam_eps = 1e-08
scale_eps = 1e-06
corr_one = 1.0 - 0.9**10
corr_two = 1.0 - 0.95**10

f32 = jnp.float32
bf16 = jnp.bfloat16


def params(mib=24):
    return pltpu.CompilerParams(vmem_limit_bytes=mib * 1024 * 1024)


def cost(flops, nbytes):
    return pl.CostEstimate(flops=flops, bytes_accessed=nbytes, transcendentals=0)


def encode(value, factor):
    size = jnp.exp(jnp.abs(value) * factor - OFFSET)
    return jnp.where(value < 0, -size, size)


def decode(code, step):
    size = (jnp.log(jnp.abs(code)) + OFFSET) * step
    return jnp.where(code < 0, -size, size)


def scale_of(peak):
    return jnp.maximum(peak * (1.0 + 2.0**-7), 1e-30).astype(bf16)


def pack_kernel(idx, v0, v1, v2, v3, scales, out, rows):
    rows[...] = scales[...].astype(f32).T
    pad = jnp.zeros((XR, BLOCK - HB), bf16)
    for k, values in enumerate((v0, v1, v2, v3)):
        start = pl.multiple_of(idx[1 + k] * XR, XR)
        block = rows[pl.ds(start, XR), :]
        chosen = jnp.where(idx[0] == 0, block[:, :HB], block[:, HB:])
        out[k, :, :HALF] = values[...]
        out[k, :, HALF : HALF + HB] = chosen.astype(bf16)
        out[k, :, HALF + HB :] = pad


def pack(idx, values, scales, name):
    values = in_hbm(values)
    rows = [
        pl.BlockSpec((XR, HALF), lambda i, s, k=k: (s[1 + k], s[0])) for k in range(NX)
    ]
    return pl.pallas_call(
        pack_kernel,
        grid_spec=pltpu.PrefetchScalarGridSpec(
            num_scalar_prefetch=1,
            grid=(1,),
            in_specs=rows + [pl.BlockSpec((NB, ROWS), lambda i, s: (0, 0))],
            out_specs=pl.BlockSpec((NX, XR, PAD), lambda i, s: (0, 0, 0)),
            scratch_shapes=[pltpu.VMEM((ROWS, NB), f32)],
        ),
        out_shape=jax.ShapeDtypeStruct((NX, XR, PAD), bf16),
        compiler_params=params(),
        cost_estimate=cost(0, 4 * ROWS * HALF * 2),
        name=name,
    )(idx, *([values] * NX), in_hbm(scales))


def in_hbm(value):
    return pltpu.with_memory_space_constraint(value, pltpu.HBM)


def add_cores(values, scales, there, there_scales, totals):
    mine = scales[...].astype(f32)
    theirs = there_scales[...].astype(f32)
    peak = jnp.zeros((XR, BLOCK), f32)
    for b in range(HB):
        cols = slice(b * BLOCK, (b + 1) * BLOCK)
        total = values[:, cols].astype(f32) * mine[:, b : b + 1]
        total = total + there[:, cols].astype(f32) * theirs[:, b : b + 1]
        totals[:, cols] = total
        peak = jnp.maximum(peak, jnp.abs(total))
    return peak


def code_kernel(values, scales, there, there_scales, out, totals):
    scale = scale_of(add_cores(values, scales, there, there_scales, totals))
    out[:, HALF:] = scale
    factor = SPAN / scale.astype(f32)
    for b in range(HB):
        cols = slice(b * BLOCK, (b + 1) * BLOCK)
        out[:, cols] = encode(totals[:, cols], factor).astype(bf16)


def own_kernel(values, scales, there, there_scales, out):
    add_cores(values, scales, there, there_scales, out)


def chip_sum(k, own, there, coded):
    if coded:
        kernel, width, kind, name = code_kernel, PAD, bf16, "coded_chip_sum"
        scratch = [pltpu.VMEM((XR, HALF), f32)]
    else:
        kernel, width, kind, name = own_kernel, HALF, f32, "own_chip_sum"
        scratch = []
    value = pl.BlockSpec((None, XR, HALF), lambda i: (k, 0, 0))
    scale = pl.BlockSpec((None, XR, BLOCK), lambda i: (k, 0, HB))
    return pl.pallas_call(
        kernel,
        grid=(1,),
        in_specs=[value, scale, value, scale],
        out_specs=pl.BlockSpec((XR, width), lambda i: (0, 0)),
        scratch_shapes=scratch,
        out_shape=jax.ShapeDtypeStruct((XR, width), kind),
        compiler_params=params(),
        cost_estimate=cost(20 * XR * HALF, 6 * XR * HALF),
        name=name,
    )(own, own, there, there)


def row_kernel(own, c1, s1, c2, s2, c3, s3, out, totals):
    coded = [
        (ref, scale[...].astype(f32) * (1.0 / SPAN))
        for ref, scale in ((c1, s1), (c2, s2), (c3, s3))
    ]
    peak = jnp.zeros((XR, BLOCK), f32)
    for b in range(HB):
        cols = slice(b * BLOCK, (b + 1) * BLOCK)
        total = own[:, cols]
        for ref, step in coded:
            total = total + decode(ref[:, cols].astype(f32), step)
        totals[:, cols] = total
        peak = jnp.maximum(peak, jnp.abs(total))
    scale = scale_of(peak).astype(f32)
    for z in range(NZ):
        planes = slice(z * NY, (z + 1) * NY)
        out[planes, :, QUARTER:] = scale.reshape(NY, YR, BLOCK).astype(bf16)
    factor = SPAN / scale
    for b in range(HB):
        cols = slice(b * BLOCK, (b + 1) * BLOCK)
        z, inner = b // QB, slice(b % QB * BLOCK, (b % QB + 1) * BLOCK)
        code = encode(totals[:, cols], factor)
        out[z * NY : (z + 1) * NY, :, inner] = code.reshape(NY, YR, BLOCK).astype(bf16)


def row_sum(own, arrived):
    ins = [pl.BlockSpec((XR, HALF), lambda i: (0, 0))]
    args = [own]
    for a in arrived:
        ins += [
            pl.BlockSpec((XR, HALF), lambda i: (0, 0)),
            pl.BlockSpec((XR, BLOCK), lambda i: (0, HB)),
        ]
        args += [a, a]
    return pl.pallas_call(
        row_kernel,
        grid=(1,),
        in_specs=ins,
        out_specs=pl.BlockSpec((NZ * NY, YR, QPAD), lambda i: (0, 0, 0)),
        scratch_shapes=[pltpu.VMEM((XR, HALF), f32)],
        out_shape=jax.ShapeDtypeStruct((NZ * NY, YR, QPAD), bf16),
        compiler_params=params(),
        cost_estimate=cost(60 * XR * HALF, 12 * XR * HALF),
        name="sum_over_x",
    )(*args)


def adam(gradient, master, first_old, second_old):
    first = beta_one * first_old + (1.0 - beta_one) * gradient
    second = beta_two * second_old + (1.0 - beta_two) * gradient * gradient
    direction = first / corr_one / (jnp.sqrt(second / corr_two) + adam_eps)
    return first, second, master - rate * direction


def low_kernel(idx, codes, steps, master, fm, fs, sm, ss, grad_out, low_out):
    def chosen(ref):
        scales = ref[...]
        parts = [scales[:, k * QB : (k + 1) * QB] for k in range(4)]
        low = jnp.where(idx[0] == 0, parts[0], parts[1])
        high = jnp.where(idx[0] == 2, parts[2], parts[3])
        return jnp.where(idx[0] < 2, low, high)

    parts = NZ * NY * YR
    step = steps[...].astype(f32).reshape(parts, BLOCK) * (1.0 / SPAN)
    fscale, sscale = chosen(fs), chosen(ss)
    for b in range(QB):
        cols = slice(b * BLOCK, (b + 1) * BLOCK)
        code = codes[:, :, cols].astype(f32).reshape(parts, BLOCK)
        term = decode(code, step).reshape(NZ * NY, YR, BLOCK)
        gradient = jnp.sum(term, axis=0)
        grad_out[:, cols] = gradient
        first_old = fm[:, cols].astype(f32) * fscale[:, b : b + 1]
        second_old = sm[:, cols].astype(f32) * sscale[:, b : b + 1]
        _, _, updated = adam(gradient, master[:, cols], first_old, second_old)
        low = updated.astype(bf16)
        for i in range(NZ * NY):
            low_out[i, :, cols] = low


def low_weights(quarter, codes, master, fm, fs, sm, ss):
    part = pl.BlockSpec((YR, QUARTER), lambda i, s: (0, s[0]))
    scale = pl.BlockSpec((YR, NB), lambda i, s: (0, 0))
    return pl.pallas_call(
        low_kernel,
        grid_spec=pltpu.PrefetchScalarGridSpec(
            num_scalar_prefetch=1,
            grid=(1,),
            in_specs=[
                pl.BlockSpec((NZ * NY, YR, QUARTER), lambda i, s: (0, 0, 0)),
                pl.BlockSpec((NZ * NY, YR, BLOCK), lambda i, s: (0, 0, QB)),
                part,
                part,
                scale,
                part,
                scale,
            ],
            out_specs=[
                pl.BlockSpec((YR, QUARTER), lambda i, s: (0, 0)),
                pl.BlockSpec((NZ * NY, YR, QUARTER), lambda i, s: (0, 0, 0)),
            ],
        ),
        out_shape=[
            jax.ShapeDtypeStruct((YR, QUARTER), f32),
            jax.ShapeDtypeStruct((NZ * NY, YR, QUARTER), bf16),
        ],
        compiler_params=params(),
        cost_estimate=cost(30 * XR * HALF, 8 * XR * HALF),
        name="sum_and_low_weights",
    )(quarter, codes, codes, master, fm, fs, sm, ss)


def old_kernel(fm, fs, sm, ss, of, os):
    for moment, scales, out in ((fm, fs, of), (sm, ss, os)):
        scale = jnp.concatenate([scales[:, :HB], scales[:, HB:]], axis=0)
        for b in range(HB):
            cols = slice(b * BLOCK, (b + 1) * BLOCK)
            halves = [moment[:, k * BLOCK : (k + 1) * BLOCK] for k in (b, b + HB)]
            both = jnp.concatenate([half.astype(f32) for half in halves], axis=0)
            out[:, cols] = both * scale[:, b : b + 1]


def old_moments(fm, fs, sm, ss):
    whole = pl.BlockSpec((YR, D), lambda i: (0, 0))
    scale = pl.BlockSpec((YR, NB), lambda i: (0, 0))
    stacked = pl.BlockSpec((2 * YR, HALF), lambda i: (0, 0))
    return pl.pallas_call(
        old_kernel,
        grid=(1,),
        in_specs=[whole, scale, whole, scale],
        out_specs=[stacked, stacked],
        out_shape=[jax.ShapeDtypeStruct((2 * YR, HALF), f32)] * 2,
        compiler_params=params(),
        cost_estimate=cost(2 * YR * D, OLD_BYTES),
        name="old_moments",
    )(fm, fs, sm, ss)


def state_kernel(
    idx, mine, other, master, fold, sold, om, of, ofs, os, oss, firsts, seconds
):
    first_half = idx[0] == 0

    def stacked(ref, b):
        halves = [ref[:, k * BLOCK : (k + 1) * BLOCK] for k in (b, b + HB)]
        return jnp.concatenate([half.astype(f32) for half in halves], axis=0)

    def store(ref, b, value):
        for k, rows in ((b, slice(0, YR)), (b + HB, slice(YR, 2 * YR))):
            ref[:, k * BLOCK : (k + 1) * BLOCK] = value[rows].astype(ref.dtype)

    lane = lax.broadcasted_iota(jnp.int32, (2 * YR, HB), 1)
    fpeaks = jnp.zeros((2 * YR, HB), f32)
    speaks = jnp.zeros((2 * YR, HB), f32)
    for b in range(HB):
        cols = slice(b * BLOCK, (b + 1) * BLOCK)
        one, two = mine[:, cols], other[:, cols]
        gradient = jnp.concatenate(
            [jnp.where(first_half, one, two), jnp.where(first_half, two, one)], axis=0
        )
        first, second, updated = adam(
            gradient, stacked(master, b), fold[:, cols], sold[:, cols]
        )
        store(om, b, updated)
        firsts[:, cols] = first
        seconds[:, cols] = second
        fpeak = jnp.max(jnp.abs(first), axis=1, keepdims=True)
        speak = jnp.max(second, axis=1, keepdims=True)
        fpeaks = jnp.where(lane == b, fpeak, fpeaks)
        speaks = jnp.where(lane == b, speak, speaks)
    fpeaks = fpeaks + scale_eps
    speaks = speaks + scale_eps
    for ref, peaks in ((ofs, fpeaks), (oss, speaks)):
        ref[:, :HB] = peaks[:YR]
        ref[:, HB:] = peaks[YR:]
    finverse, sinverse = 1.0 / fpeaks, 1.0 / speaks
    for b in range(HB):
        cols = slice(b * BLOCK, (b + 1) * BLOCK)
        store(of, b, firsts[:, cols] * finverse[:, b : b + 1])
        store(os, b, seconds[:, cols] * sinverse[:, b : b + 1])


def states(core, mine, other, master, fold, sold):
    half = pl.BlockSpec((YR, HALF), lambda i, s: (0, 0))
    whole = pl.BlockSpec((YR, D), lambda i, s: (0, 0))
    scale = pl.BlockSpec((YR, NB), lambda i, s: (0, 0))
    stacked = pl.BlockSpec((2 * YR, HALF), lambda i, s: (0, 0))
    shape = jax.ShapeDtypeStruct
    return pl.pallas_call(
        state_kernel,
        grid_spec=pltpu.PrefetchScalarGridSpec(
            num_scalar_prefetch=1,
            grid=(1,),
            in_specs=[half, half, whole, stacked, stacked],
            out_specs=[whole, whole, scale, whole, scale],
            scratch_shapes=[pltpu.VMEM((2 * YR, HALF), f32)] * 2,
        ),
        out_shape=[
            shape((YR, D), f32),
            shape((YR, D), bf16),
            shape((YR, NB), f32),
            shape((YR, D), bf16),
            shape((YR, NB), f32),
        ],
        compiler_params=params(),
        cost_estimate=cost(YR * D, YR * D),
        name="new_states",
    )(core, mine, other, master, fold, sold)


def spread_kernel(low, out):
    for z in range(NZ):
        cols = slice(z * QUARTER, (z + 1) * QUARTER)
        rows = low[z * NY : (z + 1) * NY].astype(f32).reshape(XR, QUARTER)
        for k in range(NX):
            out[k, :, cols] = rows.astype(bf16)


def spread(low):
    return pl.pallas_call(
        spread_kernel,
        grid=(1,),
        in_specs=[pl.BlockSpec((NZ * NY, YR, QUARTER), lambda i: (0, 0, 0))],
        out_specs=pl.BlockSpec((NX, XR, HALF), lambda i: (0, 0, 0)),
        out_shape=jax.ShapeDtypeStruct((NX, XR, HALF), bf16),
        compiler_params=params(),
        cost_estimate=cost(0, 10 * XR * HALF),
        name="spread_rows",
    )(low)


def place_kernel(idx, piece, *refs):
    weights, transposed = refs[-2:]
    low = piece[...].reshape(ROWS, CH)
    weights[...] = low
    transposed[...] = low.T


def place(half, piece, before=()):
    steps = HALF // CH
    return pl.pallas_call(
        place_kernel,
        grid_spec=pltpu.PrefetchScalarGridSpec(
            num_scalar_prefetch=1,
            grid=(steps,),
            in_specs=[pl.BlockSpec((NX, XR, CH), lambda j, s: (0, 0, j))]
            + [pl.BlockSpec(memory_space=pl.ANY)] * len(before),
            out_specs=[
                pl.BlockSpec((ROWS, CH), lambda j, s: (0, s[0] * steps + j)),
                pl.BlockSpec((CH, ROWS), lambda j, s: (s[0] * steps + j, 0)),
            ],
        ),
        out_shape=[
            jax.ShapeDtypeStruct((ROWS, D), bf16),
            jax.ShapeDtypeStruct((D, ROWS), bf16),
        ],
        input_output_aliases={2: 0, 3: 1} if before else {},
        compiler_params=params(),
        cost_estimate=cost(0, 3 * ROWS * HALF * 2),
        name="place_weights",
    )(half, piece, *before)


def shift_x(value, shift):
    return lax.ppermute(value, "x", [(i, (i + shift) % NX) for i in range(NX)])


def exchange(value, axis):
    return lax.all_to_all(value, axis, 0, 0, tiled=True)


def swap(value, axis):
    return lax.ppermute(value, axis, [(0, 1), (1, 0)])


def on_device(gv, gs, master, fm, fs, sm, ss):
    gv, gs = gv.reshape(ROWS, D), jnp.swapaxes(gs.reshape(ROWS, NB), 0, 1)
    master, fm, sm = master.reshape(YR, D), fm.reshape(YR, D), sm.reshape(YR, D)
    fs, ss = fs.reshape(YR, NB), ss.reshape(YR, NB)
    x = lax.axis_index("x").astype(jnp.int32)
    core = lax.axis_index("c").astype(jnp.int32)
    plane = lax.axis_index("zl").astype(jnp.int32)
    half = core.reshape(1)

    def blocks(*shifts):
        return [lax.rem(x + shift, NX) for shift in shifts]

    order = blocks(2, 1, 3, 0)
    packed = pack(jnp.stack([1 - core] + order), gv, gs, "pack_theirs")
    mine = pack(jnp.stack([core] + order), gv, gs, "pack_mine")
    there = swap(packed, "c")
    arrived = [
        shift_x(chip_sum(k, mine, there, True), shift)
        for k, shift in enumerate((2, 1, 3))
    ]
    own = chip_sum(3, mine, there, False)
    codes = exchange(row_sum(own, arrived), ("zl", "y"))
    quarter, low = low_weights(
        (2 * core + plane).reshape(1), codes, master, fm, fs, sm, ss
    )
    low_y = exchange(low, ("zl", "y"))
    quarter, fm, fs, sm, ss = lax.optimization_barrier((quarter, fm, fs, sm, ss))
    fold, sold = old_moments(fm, fs, sm, ss)

    from_z = swap(quarter, "zl")
    left = jnp.where(plane == 0, quarter, from_z)
    right = jnp.where(plane == 0, from_z, quarter)
    gradient = jnp.concatenate([left, right], axis=1)
    other_gradient = swap(gradient, "c")
    new = states(half, gradient, other_gradient, master, fold, sold)

    low_y, new = lax.optimization_barrier((low_y, new))
    near = exchange(spread(low_y), "x")
    far = swap(near, "c")
    weights, transposed = place(1 - half, far, place(half, near))
    om, of, ofs, os, oss = [a[None] for a in new]
    return om, of, ofs, os, oss, weights[None], transposed[None]


def solution(mesh):
    fine = Mesh(
        mesh.devices.reshape(NZ, 2, NX, NY, mesh.devices.shape[-1]),
        ("zl", "c", "x", "y", "zh"),
    )
    grads = P(("zl", "c"), ("x", "y"), "zh", None, None)
    rows = P("zh", ("x", "y"), None)
    shard = P("zh", None, None)
    return jax.shard_map(
        on_device,
        mesh=fine,
        in_specs=(grads, grads, rows, rows, rows, rows, rows),
        out_specs=(rows,) * 5 + (shard, shard),
        check_vma=False,
    )
```

```python
import functools

import jax
import jax.numpy as jnp
from jax import lax
from jax.experimental import pallas as pl
from jax.experimental.pallas import tpu as pltpu
from jax.sharding import Mesh, PartitionSpec as P

D = 12288
HALF = D // 2
OLD_BYTES = 24 * 1024 * 1024
BLOCK = 128
NB = D // BLOCK
HB = NB // 2
ROWS = 128
NX, NY, NZ = 4, 8, 2
XR = ROWS // NX
YR = XR // NY
QUARTER = D // 4
QB = NB // 4
PAD = HALF + BLOCK
QPAD = QUARTER + BLOCK
CH = 2048
SPAN = 172.0
OFFSET = 86.0

beta_one = 0.9
beta_two = 0.95
rate = 0.02
adam_eps = 1e-08
scale_eps = 1e-06
corr_one = 1.0 - 0.9**10
corr_two = 1.0 - 0.95**10

f32 = jnp.float32
bf16 = jnp.bfloat16


def params(mib=24):
    return pltpu.CompilerParams(vmem_limit_bytes=mib * 1024 * 1024)


def cost(flops, nbytes):
    return pl.CostEstimate(flops=flops, bytes_accessed=nbytes, transcendentals=0)


def encode(value, factor):
    size = jnp.exp(jnp.abs(value) * factor - OFFSET)
    return jnp.where(value < 0, -size, size)


def decode(code, step):
    size = (jnp.log(jnp.abs(code)) + OFFSET) * step
    return jnp.where(code < 0, -size, size)


def scale_of(peak):
    return jnp.maximum(peak * (1.0 + 2.0**-7), 1e-30).astype(bf16)


def pack_kernel(idx, v0, v1, v2, v3, scales, out, rows):
    rows[...] = scales[...].astype(f32).T
    pad = jnp.zeros((XR, BLOCK - HB), bf16)
    for k, values in enumerate((v0, v1, v2, v3)):
        start = pl.multiple_of(idx[1 + k] * XR, XR)
        block = rows[pl.ds(start, XR), :]
        chosen = jnp.where(idx[0] == 0, block[:, :HB], block[:, HB:])
        out[k, :, :HALF] = values[...]
        out[k, :, HALF : HALF + HB] = chosen.astype(bf16)
        out[k, :, HALF + HB :] = pad


def pack(idx, values, scales, name):
    values = in_hbm(values)
    rows = [
        pl.BlockSpec((XR, HALF), lambda i, s, k=k: (s[1 + k], s[0])) for k in range(NX)
    ]
    return pl.pallas_call(
        pack_kernel,
        grid_spec=pltpu.PrefetchScalarGridSpec(
            num_scalar_prefetch=1,
            grid=(1,),
            in_specs=rows + [pl.BlockSpec((NB, ROWS), lambda i, s: (0, 0))],
            out_specs=pl.BlockSpec((NX, XR, PAD), lambda i, s: (0, 0, 0)),
            scratch_shapes=[pltpu.VMEM((ROWS, NB), f32)],
        ),
        out_shape=jax.ShapeDtypeStruct((NX, XR, PAD), bf16),
        compiler_params=params(),
        cost_estimate=cost(0, 4 * ROWS * HALF * 2),
        name=name,
    )(idx, *([values] * NX), in_hbm(scales))


def in_hbm(value):
    return pltpu.with_memory_space_constraint(value, pltpu.HBM)


def add_cores(values, scales, there, there_scales, totals):
    mine = scales[...].astype(f32)
    theirs = there_scales[...].astype(f32)
    peak = jnp.zeros((XR, BLOCK), f32)
    for b in range(HB):
        cols = slice(b * BLOCK, (b + 1) * BLOCK)
        total = values[:, cols].astype(f32) * mine[:, b : b + 1]
        total = total + there[:, cols].astype(f32) * theirs[:, b : b + 1]
        totals[:, cols] = total
        peak = jnp.maximum(peak, jnp.abs(total))
    return peak


def code_kernel(values, scales, there, there_scales, out, totals):
    scale = scale_of(add_cores(values, scales, there, there_scales, totals))
    out[:, HALF:] = scale
    factor = SPAN / scale.astype(f32)
    for b in range(HB):
        cols = slice(b * BLOCK, (b + 1) * BLOCK)
        out[:, cols] = encode(totals[:, cols], factor).astype(bf16)


def own_kernel(values, scales, there, there_scales, out):
    add_cores(values, scales, there, there_scales, out)


def chip_sum(k, own, there, coded):
    if coded:
        kernel, width, kind, name = code_kernel, PAD, bf16, "coded_chip_sum"
        scratch = [pltpu.VMEM((XR, HALF), f32)]
    else:
        kernel, width, kind, name = own_kernel, HALF, f32, "own_chip_sum"
        scratch = []
    value = pl.BlockSpec((None, XR, HALF), lambda i: (k, 0, 0))
    scale = pl.BlockSpec((None, XR, BLOCK), lambda i: (k, 0, HB))
    return pl.pallas_call(
        kernel,
        grid=(1,),
        in_specs=[value, scale, value, scale],
        out_specs=pl.BlockSpec((XR, width), lambda i: (0, 0)),
        scratch_shapes=scratch,
        out_shape=jax.ShapeDtypeStruct((XR, width), kind),
        compiler_params=params(),
        cost_estimate=cost(20 * XR * HALF, 6 * XR * HALF),
        name=name,
    )(own, own, there, there)


def row_kernel(own, c1, s1, c2, s2, c3, s3, out, totals):
    coded = [
        (ref, scale[...].astype(f32) * (1.0 / SPAN))
        for ref, scale in ((c1, s1), (c2, s2), (c3, s3))
    ]
    peak = jnp.zeros((XR, BLOCK), f32)
    for b in range(HB):
        cols = slice(b * BLOCK, (b + 1) * BLOCK)
        total = own[:, cols]
        for ref, step in coded:
            total = total + decode(ref[:, cols].astype(f32), step)
        totals[:, cols] = total
        peak = jnp.maximum(peak, jnp.abs(total))
    scale = scale_of(peak).astype(f32)
    for z in range(NZ):
        planes = slice(z * NY, (z + 1) * NY)
        out[planes, :, QUARTER:] = scale.reshape(NY, YR, BLOCK).astype(bf16)
    factor = SPAN / scale
    for b in range(HB):
        cols = slice(b * BLOCK, (b + 1) * BLOCK)
        z, inner = b // QB, slice(b % QB * BLOCK, (b % QB + 1) * BLOCK)
        code = encode(totals[:, cols], factor)
        out[z * NY : (z + 1) * NY, :, inner] = code.reshape(NY, YR, BLOCK).astype(bf16)


def row_sum(own, arrived):
    ins = [pl.BlockSpec((XR, HALF), lambda i: (0, 0))]
    args = [own]
    for a in arrived:
        ins += [
            pl.BlockSpec((XR, HALF), lambda i: (0, 0)),
            pl.BlockSpec((XR, BLOCK), lambda i: (0, HB)),
        ]
        args += [a, a]
    return pl.pallas_call(
        row_kernel,
        grid=(1,),
        in_specs=ins,
        out_specs=pl.BlockSpec((NZ * NY, YR, QPAD), lambda i: (0, 0, 0)),
        scratch_shapes=[pltpu.VMEM((XR, HALF), f32)],
        out_shape=jax.ShapeDtypeStruct((NZ * NY, YR, QPAD), bf16),
        compiler_params=params(),
        cost_estimate=cost(60 * XR * HALF, 12 * XR * HALF),
        name="sum_over_x",
    )(*args)


def adam(gradient, master, first_old, second_old):
    first = beta_one * first_old + (1.0 - beta_one) * gradient
    second = beta_two * second_old + (1.0 - beta_two) * gradient * gradient
    direction = first / corr_one / (jnp.sqrt(second / corr_two) + adam_eps)
    return first, second, master - rate * direction


def low_kernel(idx, codes, steps, master, fm, fs, sm, ss, grad_out, low_out):
    def chosen(ref):
        scales = ref[...]
        parts = [scales[:, k * QB : (k + 1) * QB] for k in range(4)]
        low = jnp.where(idx[0] == 0, parts[0], parts[1])
        high = jnp.where(idx[0] == 2, parts[2], parts[3])
        return jnp.where(idx[0] < 2, low, high)

    parts = NZ * NY * YR
    step = steps[...].astype(f32).reshape(parts, BLOCK) * (1.0 / SPAN)
    fscale, sscale = chosen(fs), chosen(ss)
    for b in range(QB):
        cols = slice(b * BLOCK, (b + 1) * BLOCK)
        code = codes[:, :, cols].astype(f32).reshape(parts, BLOCK)
        term = decode(code, step).reshape(NZ * NY, YR, BLOCK)
        gradient = jnp.sum(term, axis=0)
        grad_out[:, cols] = gradient
        first_old = fm[:, cols].astype(f32) * fscale[:, b : b + 1]
        second_old = sm[:, cols].astype(f32) * sscale[:, b : b + 1]
        _, _, updated = adam(gradient, master[:, cols], first_old, second_old)
        low = updated.astype(bf16)
        for i in range(NZ * NY):
            low_out[i, :, cols] = low


def low_weights(quarter, codes, master, fm, fs, sm, ss):
    part = pl.BlockSpec((YR, QUARTER), lambda i, s: (0, s[0]))
    scale = pl.BlockSpec((YR, NB), lambda i, s: (0, 0))
    return pl.pallas_call(
        low_kernel,
        grid_spec=pltpu.PrefetchScalarGridSpec(
            num_scalar_prefetch=1,
            grid=(1,),
            in_specs=[
                pl.BlockSpec((NZ * NY, YR, QUARTER), lambda i, s: (0, 0, 0)),
                pl.BlockSpec((NZ * NY, YR, BLOCK), lambda i, s: (0, 0, QB)),
                part,
                part,
                scale,
                part,
                scale,
            ],
            out_specs=[
                pl.BlockSpec((YR, QUARTER), lambda i, s: (0, 0)),
                pl.BlockSpec((NZ * NY, YR, QUARTER), lambda i, s: (0, 0, 0)),
            ],
        ),
        out_shape=[
            jax.ShapeDtypeStruct((YR, QUARTER), f32),
            jax.ShapeDtypeStruct((NZ * NY, YR, QUARTER), bf16),
        ],
        compiler_params=params(),
        cost_estimate=cost(30 * XR * HALF, 8 * XR * HALF),
        name="sum_and_low_weights",
    )(quarter, codes, codes, master, fm, fs, sm, ss)


def old_kernel(fm, fs, sm, ss, of, os):
    for moment, scales, out in ((fm, fs, of), (sm, ss, os)):
        scale = jnp.concatenate([scales[:, :HB], scales[:, HB:]], axis=0)
        for b in range(HB):
            cols = slice(b * BLOCK, (b + 1) * BLOCK)
            halves = [moment[:, k * BLOCK : (k + 1) * BLOCK] for k in (b, b + HB)]
            both = jnp.concatenate([half.astype(f32) for half in halves], axis=0)
            out[:, cols] = both * scale[:, b : b + 1]


def old_moments(fm, fs, sm, ss):
    whole = pl.BlockSpec((YR, D), lambda i: (0, 0))
    scale = pl.BlockSpec((YR, NB), lambda i: (0, 0))
    stacked = pl.BlockSpec((2 * YR, HALF), lambda i: (0, 0))
    return pl.pallas_call(
        old_kernel,
        grid=(1,),
        in_specs=[whole, scale, whole, scale],
        out_specs=[stacked, stacked],
        out_shape=[jax.ShapeDtypeStruct((2 * YR, HALF), f32)] * 2,
        compiler_params=params(),
        cost_estimate=cost(2 * YR * D, OLD_BYTES),
        name="old_moments",
    )(fm, fs, sm, ss)


def state_kernel(
    idx, mine, other, master, fold, sold, om, of, ofs, os, oss, firsts, seconds
):
    first_half = idx[0] == 0

    def stacked(ref, b):
        halves = [ref[:, k * BLOCK : (k + 1) * BLOCK] for k in (b, b + HB)]
        return jnp.concatenate([half.astype(f32) for half in halves], axis=0)

    def store(ref, b, value):
        for k, rows in ((b, slice(0, YR)), (b + HB, slice(YR, 2 * YR))):
            ref[:, k * BLOCK : (k + 1) * BLOCK] = value[rows].astype(ref.dtype)

    lane = lax.broadcasted_iota(jnp.int32, (2 * YR, HB), 1)
    fpeaks = jnp.zeros((2 * YR, HB), f32)
    speaks = jnp.zeros((2 * YR, HB), f32)
    for b in range(HB):
        cols = slice(b * BLOCK, (b + 1) * BLOCK)
        one, two = mine[:, cols], other[:, cols]
        gradient = jnp.concatenate(
            [jnp.where(first_half, one, two), jnp.where(first_half, two, one)], axis=0
        )
        first, second, updated = adam(
            gradient, stacked(master, b), fold[:, cols], sold[:, cols]
        )
        store(om, b, updated)
        firsts[:, cols] = first
        seconds[:, cols] = second
        fpeak = jnp.max(jnp.abs(first), axis=1, keepdims=True)
        speak = jnp.max(second, axis=1, keepdims=True)
        fpeaks = jnp.where(lane == b, fpeak, fpeaks)
        speaks = jnp.where(lane == b, speak, speaks)
    fpeaks = fpeaks + scale_eps
    speaks = speaks + scale_eps
    for ref, peaks in ((ofs, fpeaks), (oss, speaks)):
        ref[:, :HB] = peaks[:YR]
        ref[:, HB:] = peaks[YR:]
    finverse, sinverse = 1.0 / fpeaks, 1.0 / speaks
    for b in range(HB):
        cols = slice(b * BLOCK, (b + 1) * BLOCK)
        store(of, b, firsts[:, cols] * finverse[:, b : b + 1])
        store(os, b, seconds[:, cols] * sinverse[:, b : b + 1])


def states(core, mine, other, master, fold, sold):
    half = pl.BlockSpec((YR, HALF), lambda i, s: (0, 0))
    whole = pl.BlockSpec((YR, D), lambda i, s: (0, 0))
    scale = pl.BlockSpec((YR, NB), lambda i, s: (0, 0))
    stacked = pl.BlockSpec((2 * YR, HALF), lambda i, s: (0, 0))
    shape = jax.ShapeDtypeStruct
    return pl.pallas_call(
        state_kernel,
        grid_spec=pltpu.PrefetchScalarGridSpec(
            num_scalar_prefetch=1,
            grid=(1,),
            in_specs=[half, half, whole, stacked, stacked],
            out_specs=[whole, whole, scale, whole, scale],
            scratch_shapes=[pltpu.VMEM((2 * YR, HALF), f32)] * 2,
        ),
        out_shape=[
            shape((YR, D), f32),
            shape((YR, D), bf16),
            shape((YR, NB), f32),
            shape((YR, D), bf16),
            shape((YR, NB), f32),
        ],
        compiler_params=params(),
        cost_estimate=cost(YR * D, YR * D),
        name="new_states",
    )(core, mine, other, master, fold, sold)


def spread_kernel(low, out):
    for z in range(NZ):
        cols = slice(z * QUARTER, (z + 1) * QUARTER)
        rows = low[z * NY : (z + 1) * NY].astype(f32).reshape(XR, QUARTER)
        for k in range(NX):
            out[k, :, cols] = rows.astype(bf16)


def spread(low):
    return pl.pallas_call(
        spread_kernel,
        grid=(1,),
        in_specs=[pl.BlockSpec((NZ * NY, YR, QUARTER), lambda i: (0, 0, 0))],
        out_specs=pl.BlockSpec((NX, XR, HALF), lambda i: (0, 0, 0)),
        out_shape=jax.ShapeDtypeStruct((NX, XR, HALF), bf16),
        compiler_params=params(),
        cost_estimate=cost(0, 10 * XR * HALF),
        name="spread_rows",
    )(low)


def place_kernel(idx, piece, *refs):
    weights, transposed = refs[-2:]
    low = piece[...].reshape(ROWS, CH)
    weights[...] = low
    transposed[...] = low.T


def place(half, piece, before=()):
    steps = HALF // CH
    return pl.pallas_call(
        place_kernel,
        grid_spec=pltpu.PrefetchScalarGridSpec(
            num_scalar_prefetch=1,
            grid=(steps,),
            in_specs=[pl.BlockSpec((NX, XR, CH), lambda j, s: (0, 0, j))]
            + [pl.BlockSpec(memory_space=pl.ANY)] * len(before),
            out_specs=[
                pl.BlockSpec((ROWS, CH), lambda j, s: (0, s[0] * steps + j)),
                pl.BlockSpec((CH, ROWS), lambda j, s: (s[0] * steps + j, 0)),
            ],
        ),
        out_shape=[
            jax.ShapeDtypeStruct((ROWS, D), bf16),
            jax.ShapeDtypeStruct((D, ROWS), bf16),
        ],
        input_output_aliases={2: 0, 3: 1} if before else {},
        compiler_params=params(),
        cost_estimate=cost(0, 3 * ROWS * HALF * 2),
        name="place_weights",
    )(half, piece, *before)


def shift_x(value, shift):
    return lax.ppermute(value, "x", [(i, (i + shift) % NX) for i in range(NX)])


def exchange(value, axis):
    return lax.all_to_all(value, axis, 0, 0, tiled=True)


def swap(value, axis):
    return lax.ppermute(value, axis, [(0, 1), (1, 0)])


def on_device(gv, gs, master, fm, fs, sm, ss):
    gv, gs = gv.reshape(ROWS, D), jnp.swapaxes(gs.reshape(ROWS, NB), 0, 1)
    master, fm, sm = master.reshape(YR, D), fm.reshape(YR, D), sm.reshape(YR, D)
    fs, ss = fs.reshape(YR, NB), ss.reshape(YR, NB)
    x = lax.axis_index("x").astype(jnp.int32)
    core = lax.axis_index("c").astype(jnp.int32)
    plane = lax.axis_index("zl").astype(jnp.int32)
    half = core.reshape(1)

    def blocks(*shifts):
        return [lax.rem(x + shift, NX) for shift in shifts]

    order = blocks(2, 1, 3, 0)
    packed = pack(jnp.stack([1 - core] + order), gv, gs, "pack_theirs")
    mine = pack(jnp.stack([core] + order), gv, gs, "pack_mine")
    there = swap(packed, "c")
    arrived = [
        shift_x(chip_sum(k, mine, there, True), shift)
        for k, shift in enumerate((2, 1, 3))
    ]
    own = chip_sum(3, mine, there, False)
    codes = exchange(row_sum(own, arrived), ("zl", "y"))
    quarter, low = low_weights(
        (2 * core + plane).reshape(1), codes, master, fm, fs, sm, ss
    )
    low_y = exchange(low, ("zl", "y"))
    quarter, fm, fs, sm, ss = lax.optimization_barrier((quarter, fm, fs, sm, ss))
    fold, sold = old_moments(fm, fs, sm, ss)

    from_z = swap(quarter, "zl")
    left = jnp.where(plane == 0, quarter, from_z)
    right = jnp.where(plane == 0, from_z, quarter)
    gradient = jnp.concatenate([left, right], axis=1)
    other_gradient = swap(gradient, "c")
    new = states(half, gradient, other_gradient, master, fold, sold)

    low_y, new = lax.optimization_barrier((low_y, new))
    near = exchange(spread(low_y), "x")
    far = swap(near, "c")
    weights, transposed = place(1 - half, far, place(half, near))
    om, of, ofs, os, oss = [a[None] for a in new]
    return om, of, ofs, os, oss, weights[None], transposed[None]


def solution(mesh):
    fine = Mesh(
        mesh.devices.reshape(NZ, 2, NX, NY, mesh.devices.shape[-1]),
        ("zl", "c", "x", "y", "zh"),
    )
    grads = P(("zl", "c"), ("x", "y"), "zh", None, None)
    rows = P("zh", ("x", "y"), None)
    shard = P("zh", None, None)
    return jax.shard_map(
        on_device,
        mesh=fine,
        in_specs=(grads, grads, rows, rows, rows, rows, rows),
        out_specs=(rows,) * 5 + (shard, shard),
        check_vma=False,
    )
```
